256 devices in a mesh: chan: 32 (over z, y_lo, core), win: 8 (over y_hi, x).
Axes of the slice: x: 4, y: 4 (y_hi: 2, y_lo: 2; y = y_hi * 2 + y_lo), z: 8, core: 2. Of those that a mesh axis runs over, the one named last changes fastest.
Arguments:
- recordings: bfloat16 [8, 256, 4096], P('win', 'chan'), may hold values from -6 to 6
- channel_live: int32 [256], P('chan'), may hold values 0 or 1
Outputs:
- correlations: float32 [128, 256, 128], P('win', 'chan')
The draws below stay inside these ranges and needn't reach their ends.
All inputs are finite; a program needn't handle non-finite values. No bound on the sum of `channel_live` on one device may be relied on, other than what follows from the above.
Results may differ from the reference program's by a relative error of at most 0.017.
Values may be sent and summed in bfloat16 or wider, within the bound.
A program may use at most 128 MiB of HBM per device.

```python
import math
import jax
import jax.numpy as jnp
from jax import lax

NF = 2048
NT = 4096
WB = 64
BAND = 128
LAGS = 128
CHANNELS = 256
WINDOWS = 8


def set_ends(values, rng, low, high):
    index_at = [jax.random.randint(jax.random.fold_in(rng, axis), (), 0, length) for axis, length in enumerate(values.shape)]
    widest = values.shape.index(max(values.shape))
    next_to = index_at[:widest] + [(index_at[widest] + 1) % values.shape[widest]] + index_at[widest + 1:]
    return values.at[tuple(index_at)].set(low).at[tuple(next_to)].set(high)


def block_scale(rng, dims, pieces, least, top_value):
    loudness = 1.0
    for dim, shards_of in pieces:
        steps = jax.random.uniform(jax.random.fold_in(jax.random.fold_in(rng, 6), dim), (shards_of,), jnp.float32, least / len(pieces), top_value / len(pieces))
        loudness = loudness * jnp.repeat(jnp.exp(steps), dims[dim] // shards_of).reshape((-1,) + (1,) * (len(dims) - 1 - dim))
    return loudness


def noise(key, shape, deviation, most, pieces=(), held_as=jnp.bfloat16):
    drawn = jax.random.normal(key, shape, jnp.float32) * deviation
    if len(pieces) > 0:
        drawn = block_scale(key, shape, pieces, -0.22, 0.18) * drawn
    return jnp.clip(drawn, min=-most, max=most).astype(held_as)


def setup_inputs(seed: int = 0) -> dict:
    key_list = jax.random.split(jax.random.key(seed), 3)
    recordings = noise(key_list[0], (WINDOWS, CHANNELS, NT), 1.0, 6.0, ((0, 8), (1, 32)))
    channel_live = set_ends((jax.random.randint(key_list[1], (CHANNELS,), 0, 8) < 7).astype(jnp.int32), jax.random.fold_in(key_list[1], 1), 0, 1)
    return dict(recordings=recordings, channel_live=channel_live)


def forward_block(samples_flat, first_bin, block_width, sample_count):
    sample_index = lax.broadcasted_iota(jnp.int32, (sample_count, block_width), 0)
    bin_index = lax.broadcasted_iota(jnp.int32, (sample_count, block_width), 1) + first_bin
    angles = (sample_index * bin_index % sample_count).astype(jnp.float32) * (2.0 * math.pi / sample_count)
    table_block = jnp.concatenate([jnp.cos(angles), -jnp.sin(angles)], axis=1).astype(jnp.bfloat16)
    return jnp.dot(samples_flat, table_block, preferred_element_type=jnp.float32)

def inverse_table(bin_count, sample_count, lag_count, factor):
    bin_index = lax.broadcasted_iota(jnp.int32, (bin_count, lag_count), 0)
    lag_index = lax.broadcasted_iota(jnp.int32, (bin_count, lag_count), 1) - lag_count // 2
    angles = (bin_index * lag_index % sample_count).astype(jnp.float32) * (2.0 * math.pi / sample_count)
    return jnp.stack([jnp.cos(angles) * factor, -jnp.sin(angles) * factor], axis=0)

def whiten(spec_re, spec_im, channel_live, block_bins):
    leading = spec_re.shape[:-1]
    bin_count = spec_re.shape[-1]
    energy = (spec_re * spec_re + spec_im * spec_im).reshape(leading + (bin_count // block_bins, block_bins))
    amplitude = jnp.sqrt(lax.optimization_barrier(jnp.mean(energy, axis=-1, keepdims=True)) + 1e-06)
    inverse_amp = jnp.broadcast_to(1.0 / amplitude, energy.shape).reshape(leading + (bin_count,))
    factor = inverse_amp * channel_live.astype(jnp.float32)[None, :, None]
    return jnp.stack([spec_re * factor, spec_im * factor], axis=2).astype(jnp.bfloat16)

def reference(recordings, channel_live):
    samples_flat = recordings.reshape(WINDOWS * CHANNELS, NT)
    spectra = forward_block(samples_flat, 0, NF, NT)
    spec_re = spectra[:, :NF].reshape(WINDOWS, CHANNELS, NF)
    spec_im = spectra[:, NF:].reshape(WINDOWS, CHANNELS, NF)
    whitened = whiten(spec_re, spec_im, channel_live, WB)
    half_band = BAND // 2
    padded = jnp.pad(whitened, ((0, 0), (half_band, half_band), (0, 0), (0, 0)))
    lag_table = inverse_table(NF, NT, LAGS, 1.0 / math.sqrt(WINDOWS * NF)).reshape(2 * NF, LAGS).astype(jnp.bfloat16)
    own_block = whitened.astype(jnp.float32)

    def one_offset(offset_index):
        position = (offset_index + (offset_index >= half_band).astype(jnp.int32)).astype(jnp.int32)
        partner = lax.dynamic_slice_in_dim(padded, position, CHANNELS, 1).astype(jnp.float32)
        cross_re = own_block[:, :, 0] * partner[:, :, 0] + own_block[:, :, 1] * partner[:, :, 1]
        cross_im = own_block[:, :, 1] * partner[:, :, 0] - own_block[:, :, 0] * partner[:, :, 1]
        joined = jnp.concatenate([cross_re, cross_im], axis=-1).astype(jnp.bfloat16)
        return jnp.einsum('wck,kl->cl', joined, lag_table, preferred_element_type=jnp.float32)
    return lax.map(one_offset, jnp.arange(BAND, dtype=jnp.int32))
```

```python
import math

import jax
import jax.numpy as jnp
import numpy as np
from jax import lax
from jax.experimental import pallas as pl
from jax.experimental.pallas import tpu as pltpu
from jax.sharding import PartitionSpec as P

NT = 4096
NF = 2048
WB = 64
BAND = 128
LAGS = 128
C = 8
N1 = 16
N2 = 256
K1 = 16
K2 = 128
REACH = BAND // 2 // C
SLOTS = 2 * REACH + 1
MESH = pl.DeviceIdType.MESH


def bin_order():
    lane = np.arange(K2)
    return 4 * (lane % 32) + lane // 32


def tables(window_count):
    tau = 2.0 * math.pi
    k1, n1, n2 = np.arange(K1), np.arange(N1), np.arange(N2)
    k2 = bin_order()
    first = tau * (np.outer(k1, n1) % 16) / 16.0
    first = np.concatenate([np.cos(first), -np.sin(first)], axis=0)
    first = np.kron(first, np.eye(C))
    twiddle = tau * (np.outer(k1, n2) % NT) / NT
    twiddle = np.stack([np.cos(twiddle), -np.sin(twiddle)])
    twiddle = np.repeat(twiddle, C, axis=1)
    second = tau * (np.outer(n2, k2) % N2) / N2
    cos, sin = np.cos(second), np.sin(second)
    second = np.block([[cos, -sin], [sin, cos]])
    bins = k1[:, None] + K1 * k2[None, :]
    lag = tau * ((bins[:, :, None] * (np.arange(LAGS) - LAGS // 2)) % NT) / NT
    factor = 1.0 / math.sqrt(window_count * NF)
    lag = np.concatenate([np.cos(lag) * factor, -np.sin(lag) * factor], axis=1)
    return (
        jnp.asarray(first, jnp.bfloat16),
        jnp.asarray(twiddle, jnp.float32),
        jnp.asarray(second, jnp.bfloat16),
        jnp.asarray(lag, jnp.bfloat16),
    )


def kernel(
    chans,
    wins,
    live_ref,
    x_ref,
    first_ref,
    twiddle_ref,
    second_ref,
    lag_ref,
    out_ref,
    halo,
    ownb,
    acc,
    sums_out,
    sums_in,
    halo_send,
    halo_recv,
    sums_send,
    sums_recv,
):
    j = lax.axis_index("chan")
    w = lax.axis_index("win")
    group = BAND // wins

    barrier = pltpu.get_barrier_semaphore()
    for d in range(1, REACH + 1):
        for there in (j - d, j + d):

            @pl.when((there >= 0) & (there < chans))
            def _():
                pl.semaphore_signal(
                    barrier, inc=1, device_id={"chan": there}, device_id_type=MESH
                )

    for d in range(1, wins):
        pl.semaphore_signal(
            barrier, inc=1, device_id={"win": lax.rem(w + d, wins)}, device_id_type=MESH
        )

    x = x_ref[0].astype(jnp.float32)
    pieces = jnp.concatenate([x[:, N2 * n1 : N2 * (n1 + 1)] for n1 in range(N1)], axis=0)
    s = jnp.dot(first_ref[...], pieces.astype(jnp.bfloat16), preferred_element_type=jnp.float32)
    s_re, s_im = s[: K1 * C], s[K1 * C :]
    t_re, t_im = twiddle_ref[0], twiddle_ref[1]
    y = jnp.concatenate([s_re * t_re - s_im * t_im, s_re * t_im + s_im * t_re], axis=1)
    spec = jnp.dot(y.astype(jnp.bfloat16), second_ref[...], preferred_element_type=jnp.float32)
    energy = spec[:, :K2] * spec[:, :K2] + spec[:, K2:] * spec[:, K2:]
    energy = jnp.sum(energy.reshape(K1, C, K2), axis=0)
    energy = energy + pltpu.roll(energy, 64, 1)
    energy = energy + pltpu.roll(energy, 32, 1)
    row = lax.broadcasted_iota(jnp.int32, (C, K2), 0)
    live = jnp.zeros((C, K2), jnp.float32)
    for c in range(C):
        live = jnp.where(row == c, live_ref[c].astype(jnp.float32), live)
    factor = (1.0 / jnp.sqrt(energy * (1.0 / WB) + 1e-6)) * live
    factor = jnp.broadcast_to(factor[None], (K1, C, K2)).reshape(K1 * C, K2)
    white_re = (spec[:, :K2] * factor).astype(jnp.bfloat16)
    white_im = (spec[:, K2:] * factor).astype(jnp.bfloat16)
    halo[REACH, 0] = white_re
    halo[REACH, 1] = white_im

    present = jnp.minimum(j, REACH) + jnp.minimum(chans - 1 - j, REACH)
    pl.semaphore_wait(barrier, present + (wins - 1))

    def halo_copy(slot, there):
        return pltpu.make_async_remote_copy(
            src_ref=halo.at[REACH],
            dst_ref=halo.at[slot],
            send_sem=halo_send.at[slot],
            recv_sem=halo_recv.at[slot],
            device_id={"chan": there},
            device_id_type=MESH,
        )

    for d in range(1, REACH + 1):
        for sign in (-1, 1):
            there = j + sign * d
            slot = REACH - sign * d

            @pl.when((there >= 0) & (there < chans))
            def _():
                halo_copy(slot, there).start()

            @pl.when((j - sign * d < 0) | (j - sign * d >= chans))
            def _():
                halo[slot] = jnp.zeros((2, K1 * C, K2), jnp.bfloat16)

    ownb[0] = jnp.broadcast_to(
        white_re.astype(jnp.float32)[:, None, :], (K1 * C, 8, K2)
    )
    ownb[1] = jnp.broadcast_to(
        white_im.astype(jnp.float32)[:, None, :], (K1 * C, 8, K2)
    )

    def cross_terms(slots):
        total = jnp.zeros((64 * len(slots), LAGS), jnp.float32)
        for pair in range(K1 // 2):
            rows = slice(16 * pair, 16 * pair + 16)
            blocks = [
                (
                    halo[slot, 0, rows].astype(jnp.float32),
                    halo[slot, 1, rows].astype(jnp.float32),
                )
                for slot in slots
            ]
            for half in (0, 1):
                k1 = 2 * pair + half
                own_re, own_im = ownb[0, C * k1 : C * k1 + C], ownb[1, C * k1 : C * k1 + C]
                parts = []
                for block_re, block_im in blocks:
                    p_re = block_re[8 * half : 8 * half + 8][None]
                    p_im = block_im[8 * half : 8 * half + 8][None]
                    re = own_re * p_re + own_im * p_im
                    im = own_im * p_re - own_re * p_im
                    parts.append(
                        jnp.concatenate([re.reshape(64, K2), im.reshape(64, K2)], axis=1)
                    )
                cross = jnp.concatenate(parts, axis=0).astype(jnp.bfloat16)
                total += jnp.dot(cross, lag_ref[k1], preferred_element_type=jnp.float32)
        for index, slot in enumerate(slots):
            for c in range(C):
                value = total[64 * index + 8 * c : 64 * index + 8 * c + 8]
                acc[pl.ds(8 * slot + 7 - c, 8), c, :] = value

    def group_start(g):
        return group * g + 7 + (g >= wins // 2).astype(jnp.int32)

    def sums_copy(g):
        return pltpu.make_async_remote_copy(
            src_ref=sums_out.at[g],
            dst_ref=sums_in.at[w],
            send_sem=sums_send.at[g],
            recv_sem=sums_recv.at[w],
            device_id={"win": g},
            device_id_type=MESH,
        )

    cross_terms([REACH])

    def step(index, _):
        for d in (2 * index + 1, 2 * index + 2):
            for sign in (-1, 1):

                @pl.when((j + sign * d >= 0) & (j + sign * d < chans))
                def _():
                    halo_copy(REACH + sign * d, j).wait_recv()

            cross_terms([REACH - d, REACH + d])
        for g in (wins // 2 - 1 - index, wins // 2 + index):

            @pl.when(g != w)
            def _():
                value = acc[pl.ds(group_start(g), group)]
                sums_out[g] = value.reshape(group * C, LAGS).astype(jnp.bfloat16)
                sums_copy(g).start()

        return 0

    lax.fori_loop(0, wins // 2, step, 0)

    out_ref[...] = acc[pl.ds(group_start(w), group)]

    def gather(step, _):
        source = lax.rem(w + step, wins)
        pltpu.make_async_remote_copy(
            src_ref=sums_out.at[source],
            dst_ref=sums_in.at[source],
            send_sem=sums_send.at[source],
            recv_sem=sums_recv.at[source],
            device_id={"win": source},
            device_id_type=MESH,
        ).wait_recv()
        out_ref[...] += sums_in[source].astype(jnp.float32).reshape(group, C, LAGS)
        return 0

    lax.fori_loop(1, wins, gather, 0)

    for g in range(wins):

        @pl.when(g != w)
        def _():
            sums_copy(g).wait_send()

    for d in range(1, REACH + 1):
        for sign in (-1, 1):

            @pl.when((j + sign * d >= 0) & (j + sign * d < chans))
            def _():
                halo_copy(REACH - sign * d, j + sign * d).wait_send()


def solution(mesh):
    chans, wins = mesh.shape["chan"], mesh.shape["win"]
    group = BAND // wins

    def local(recordings, channel_live):
        first, twiddle, second, lag = tables(wins * recordings.shape[0])
        vmem = pl.BlockSpec(memory_space=pltpu.VMEM)

        def body(*refs):
            kernel(chans, wins, *refs)

        return pl.pallas_call(
            body,
            out_shape=jax.ShapeDtypeStruct((group, C, LAGS), jnp.float32),
            in_specs=[pl.BlockSpec(memory_space=pltpu.SMEM)] + [vmem] * 5,
            out_specs=vmem,
            scratch_shapes=[
                pltpu.VMEM((SLOTS, 2, K1 * C, K2), jnp.bfloat16),
                pltpu.VMEM((2, K1 * C, 8, K2), jnp.float32),
                pltpu.VMEM((8 * SLOTS + 7, C, LAGS), jnp.float32),
                pltpu.VMEM((wins, group * C, LAGS), jnp.bfloat16),
                pltpu.VMEM((wins, group * C, LAGS), jnp.bfloat16),
                pltpu.SemaphoreType.DMA((SLOTS,)),
                pltpu.SemaphoreType.DMA((SLOTS,)),
                pltpu.SemaphoreType.DMA((wins,)),
                pltpu.SemaphoreType.DMA((wins,)),
            ],
            compiler_params=pltpu.CompilerParams(
                collective_id=0, has_side_effects=True, vmem_limit_bytes=24 * 1024 * 1024
            ),
            name="correlate",
        )(channel_live, recordings, first, twiddle, second, lag)

    return jax.shard_map(
        local,
        mesh=mesh,
        in_specs=(P("win", "chan", None), P("chan")),
        out_specs=P("win", "chan", None),
        check_vma=False,
    )
```

```python
import math

import jax
import jax.numpy as jnp
import numpy as np
from jax import lax
from jax.experimental import pallas as pl
from jax.experimental.pallas import tpu as pltpu
from jax.sharding import PartitionSpec as P

NT = 4096
NF = 2048
WB = 64
BAND = 128
LAGS = 128
C = 8
N1 = 16
N2 = 256
K1 = 16
K2 = 128
PLANE = 4
PLANES = 5
SLOTS = PLANE * PLANES
UP, DOWN, SIDE, CORE = range(4)
MESH = pl.DeviceIdType.MESH


def bin_order():
    lane = np.arange(K2)
    return 4 * (lane % 32) + lane // 32


def tables(window_count):
    tau = 2.0 * math.pi
    k1, n1, n2 = np.arange(K1), np.arange(N1), np.arange(N2)
    k2 = bin_order()
    first = tau * (np.outer(k1, n1) % 16) / 16.0
    first = np.concatenate([np.cos(first), -np.sin(first)], axis=0)
    first = np.kron(first, np.eye(C))
    twiddle = tau * (np.outer(k1, n2) % NT) / NT
    twiddle = np.stack([np.cos(twiddle), -np.sin(twiddle)])
    twiddle = np.repeat(twiddle, C, axis=1)
    second = tau * (np.outer(n2, k2) % N2) / N2
    cos, sin = np.cos(second), np.sin(second)
    second = np.stack([np.concatenate([cos, sin]), np.concatenate([-sin, cos])])
    bins = k1[:, None] + K1 * k2[None, :]
    lag = tau * ((bins[:, :, None] * (np.arange(LAGS) - LAGS // 2)) % NT) / NT
    factor = 1.0 / math.sqrt(window_count * NF)
    lag = np.concatenate([np.cos(lag) * factor, -np.sin(lag) * factor], axis=1)
    return (
        jnp.asarray(first, jnp.bfloat16),
        jnp.asarray(twiddle, jnp.float32),
        jnp.asarray(second, jnp.bfloat16),
        jnp.asarray(lag, jnp.bfloat16),
    )


def kernel(
    chans,
    wins,
    live_hbm,
    x_hbm,
    first_hbm,
    twiddle_hbm,
    second_hbm,
    lag_hbm,
    out_ref,
    live_ref,
    x_ref,
    first_ref,
    twiddle_ref,
    second_ref,
    lag_ref,
    halo,
    ownb,
    acc,
    sums_out,
    sums_in,
    fetch_sem,
    halo_send,
    halo_recv,
    sums_send,
    sums_recv,
):
    j = lax.axis_index("chan")
    w = lax.axis_index("win")
    group = BAND // wins
    planes = chans // PLANE
    z, r = j // PLANE, j % PLANE
    y, core = r // 2, r % 2
    other = 1 - core
    column, beside = 2 * y, 2 - 2 * y
    own = 2 * PLANE + r

    fetches = [
        pltpu.make_async_copy(source, target, fetch_sem.at[index])
        for index, (source, target) in enumerate(
            (
                (x_hbm, x_ref),
                (first_hbm, first_ref),
                (twiddle_hbm, twiddle_ref),
                (second_hbm, second_ref),
                (live_hbm, live_ref),
                (lag_hbm, lag_ref),
            )
        )
    ]
    for fetch in fetches:
        fetch.start()

    def exists(plane):
        there = z + plane - 2
        return (there >= 0) & (there < planes)

    neighbours = {
        UP: (j + PLANE, -PLANE),
        DOWN: (j - PLANE, PLANE),
        SIDE: (j + 2 - 4 * y, 0),
        CORE: (j + 1 - 2 * core, 0),
    }

    barrier = pltpu.get_barrier_semaphore()

    def greet(there):
        pl.semaphore_signal(barrier, inc=1, device_id=there, device_id_type=MESH)

    pl.when(exists(3))(lambda: greet({"chan": j + PLANE}))
    pl.when(exists(1))(lambda: greet({"chan": j - PLANE}))
    greet({"chan": neighbours[SIDE][0]})
    greet({"chan": neighbours[CORE][0]})
    for d in range(1, wins):
        greet({"win": lax.rem(w + d, wins)})

    fetches[0].wait()
    fetches[1].wait()
    x = x_ref[0].astype(jnp.float32)
    pieces = jnp.concatenate([x[:, N2 * n1 : N2 * (n1 + 1)] for n1 in range(N1)], axis=0)
    s = jnp.dot(first_ref[...], pieces.astype(jnp.bfloat16), preferred_element_type=jnp.float32)
    s_re, s_im = s[: K1 * C], s[K1 * C :]
    fetches[2].wait()
    fetches[3].wait()
    t_re, t_im = twiddle_ref[0], twiddle_ref[1]
    y_re = (s_re * t_re - s_im * t_im).astype(jnp.bfloat16)
    y_im = (s_re * t_im + s_im * t_re).astype(jnp.bfloat16)
    spec = jnp.dot(
        jnp.concatenate([y_re, y_im], axis=1),
        jnp.concatenate([second_ref[0], second_ref[1]], axis=1),
        preferred_element_type=jnp.float32,
    )
    energy = spec[:, :K2] * spec[:, :K2] + spec[:, K2:] * spec[:, K2:]
    energy = jnp.sum(energy.reshape(K1, C, K2), axis=0)
    energy = energy + pltpu.roll(energy, 64, 1)
    energy = energy + pltpu.roll(energy, 32, 1)
    row = lax.broadcasted_iota(jnp.int32, (C, K2), 0)
    live = jnp.zeros((C, K2), jnp.float32)
    fetches[4].wait()
    for c in range(C):
        live = jnp.where(row == c, live_ref[c].astype(jnp.float32), live)
    factor = (1.0 / jnp.sqrt(energy * (1.0 / WB) + 1e-6)) * live
    factor = jnp.broadcast_to(factor[None], (K1, C, K2)).reshape(K1 * C, K2)
    white_re = (spec[:, :K2] * factor).astype(jnp.bfloat16)
    white_im = (spec[:, K2:] * factor).astype(jnp.bfloat16)
    halo[own, 0] = white_re
    halo[own, 1] = white_im

    beyond = exists(1).astype(jnp.int32) + exists(3).astype(jnp.int32)
    pl.semaphore_wait(barrier, beyond + 2 + (wins - 1))

    def halo_copy(way, slot):
        there, shift = neighbours[way]
        return pltpu.make_async_remote_copy(
            src_ref=halo.at[slot],
            dst_ref=halo.at[slot + shift],
            send_sem=halo_send.at[way, slot],
            recv_sem=halo_recv.at[slot + shift],
            device_id={"chan": there},
            device_id_type=MESH,
        )

    always = j >= 0
    has = [exists(plane) for plane in range(PLANES)]
    inside = has[1] & has[3]
    same, across = column + core, beside + core
    slot_of = [[PLANE * plane + rank for rank in (same, column + other, across, beside + other)] for plane in range(PLANES)]
    SAME, MATE, ACROSS, ACROSS_MATE = range(4)
    plan = {
        (UP, 2, SAME): has[3],
        (DOWN, 2, SAME): has[1],
        (SIDE, 2, SAME): always,
        (CORE, 2, SAME): always,
        (UP, 2, ACROSS): has[3],
        (DOWN, 2, ACROSS): has[1],
        (CORE, 2, ACROSS): always,
        (UP, 1, SAME): inside,
        (CORE, 1, SAME): has[1],
        (DOWN, 3, SAME): inside,
        (CORE, 3, SAME): has[3],
        (UP, 1, ACROSS): inside & (y == 0),
        (CORE, 1, ACROSS): has[1],
        (DOWN, 3, ACROSS): inside & (y == 1),
        (CORE, 3, ACROSS): has[3],
        (CORE, 0, SAME): has[0] & (core == 1),
        (CORE, 4, SAME): has[4] & (core == 0),
        (CORE, 0, ACROSS): has[0] & (y == 0),
        (CORE, 4, ACROSS): has[4] & (y == 1),
    }
    arrivals = {(plane, rank): has[plane] for plane in (1, 3) for rank in range(4)}
    arrivals |= {(2, rank): always for rank in (MATE, ACROSS, ACROSS_MATE)}
    arrivals |= {
        (0, SAME): has[0],
        (4, SAME): has[4],
        (0, MATE): has[0] & (core == 0),
        (4, MATE): has[4] & (core == 1),
        (0, ACROSS): has[0] & (y == 0),
        (4, ACROSS): has[4] & (y == 1),
        (0, ACROSS_MATE): has[0] & (y == 0),
        (4, ACROSS_MATE): has[4] & (y == 1),
    }

    def send(*key):
        way, plane, rank = key
        pl.when(plan[key])(lambda: halo_copy(way, slot_of[plane][rank]).start())

    def arrive(plane, rank):
        slot = slot_of[plane][rank]

        @pl.when(arrivals[plane, rank])
        def _():
            pltpu.make_async_remote_copy(
                src_ref=halo.at[slot],
                dst_ref=halo.at[slot],
                send_sem=halo_send.at[CORE, slot],
                recv_sem=halo_recv.at[slot],
                device_id={"chan": neighbours[CORE][0]},
                device_id_type=MESH,
            ).wait_recv()

    send(UP, 2, SAME)
    send(DOWN, 2, SAME)
    send(SIDE, 2, SAME)
    send(CORE, 2, SAME)

    for plane in (0, 1, 3, 4):

        @pl.when(jnp.logical_not(exists(plane)))
        def _():
            def clear(rank, _):
                halo[PLANE * plane + rank] = jnp.zeros((2, K1 * C, K2), jnp.bfloat16)
                return 0

            lax.fori_loop(0, PLANE, clear, 0)

    ownb[0] = jnp.broadcast_to(white_re.astype(jnp.float32)[:, None, :], (K1 * C, 8, K2))
    ownb[1] = jnp.broadcast_to(white_im.astype(jnp.float32)[:, None, :], (K1 * C, 8, K2))
    fetches[5].wait()

    def cross_terms(slots):
        total = jnp.zeros((64 * len(slots), LAGS), jnp.float32)
        for pair in range(K1 // 2):
            rows = slice(16 * pair, 16 * pair + 16)
            blocks = [
                (
                    halo[slot, 0, rows].astype(jnp.float32),
                    halo[slot, 1, rows].astype(jnp.float32),
                )
                for slot in slots
            ]
            for half in (0, 1):
                k1 = 2 * pair + half
                own_re, own_im = ownb[0, C * k1 : C * k1 + C], ownb[1, C * k1 : C * k1 + C]
                parts = []
                for block_re, block_im in blocks:
                    p_re = block_re[8 * half : 8 * half + 8][None]
                    p_im = block_im[8 * half : 8 * half + 8][None]
                    re = own_re * p_re + own_im * p_im
                    im = own_im * p_re - own_re * p_im
                    parts.append(
                        jnp.concatenate([re.reshape(64, K2), im.reshape(64, K2)], axis=1)
                    )
                cross = jnp.concatenate(parts, axis=0).astype(jnp.bfloat16)
                total += jnp.dot(cross, lag_ref[k1], preferred_element_type=jnp.float32)
        for index, slot in enumerate(slots):
            for c in range(C):
                value = total[64 * index + 8 * c : 64 * index + 8 * c + 8]
                acc[pl.ds(8 * (slot - r) + 7 - c, 8), c, :] = value

    def group_start(g):
        return group * g + 7 + (g >= wins // 2).astype(jnp.int32)

    def sums_copy(g):
        return pltpu.make_async_remote_copy(
            src_ref=sums_out.at[g],
            dst_ref=sums_in.at[w],
            send_sem=sums_send.at[g],
            recv_sem=sums_recv.at[w],
            device_id={"win": g},
            device_id_type=MESH,
        )

    def send_sums(first_group, count):
        def one(index, _):
            g = lax.rem(first_group + lax.rem(w + index, count), wins)

            @pl.when(g != w)
            def _():
                value = acc[pl.ds(group_start(g), group)]
                sums_out[g] = value.reshape(group * C, LAGS).astype(jnp.bfloat16)
                sums_copy(g).start()

            return 0

        lax.fori_loop(0, count, one, 0)

    far = [r + q + 12 * (r + q >= PLANE).astype(jnp.int32) for q in range(5)]
    units = [
        (own, own),
        (slot_of[2][MATE], slot_of[2][ACROSS]),
        (slot_of[2][ACROSS_MATE], slot_of[1][SAME]),
        (slot_of[3][SAME], slot_of[1][MATE]),
        (slot_of[3][MATE], slot_of[1][ACROSS]),
        (slot_of[3][ACROSS], slot_of[1][ACROSS_MATE]),
        (slot_of[3][ACROSS_MATE], far[0]),
        (far[1], far[2]),
        (far[3], far[4]),
    ]

    def before_1():
        arrive(2, ACROSS)
        send(UP, 2, ACROSS)
        send(DOWN, 2, ACROSS)
        send(CORE, 2, ACROSS)
        arrive(2, MATE)

    def before_2():
        arrive(1, SAME)
        send(UP, 1, SAME)
        send(CORE, 1, SAME)
        arrive(3, SAME)
        send(DOWN, 3, SAME)
        send(CORE, 3, SAME)
        arrive(2, ACROSS_MATE)

    def before_3():
        arrive(1, MATE)

    def before_4():
        arrive(1, ACROSS)
        send(UP, 1, ACROSS)
        send(CORE, 1, ACROSS)
        arrive(3, ACROSS)
        send(DOWN, 3, ACROSS)
        send(CORE, 3, ACROSS)
        arrive(3, MATE)

    def before_5():
        arrive(1, ACROSS_MATE)

    def before_6():
        arrive(0, SAME)
        send(CORE, 0, SAME)
        arrive(4, SAME)
        send(CORE, 4, SAME)
        arrive(3, ACROSS_MATE)
        arrive(0, MATE)
        arrive(0, ACROSS)

    def before_7():
        send(CORE, 0, ACROSS)
        arrive(4, ACROSS)
        send(CORE, 4, ACROSS)
        send_sums(2 - y, 5)
        arrive(4, MATE)
        arrive(0, ACROSS_MATE)
        arrive(4, ACROSS_MATE)

    events = {
        1: before_1,
        2: before_2,
        3: before_3,
        4: before_4,
        5: before_5,
        6: before_6,
        7: before_7,
    }

    def pick(u, values):
        chosen = values[0]
        for index in range(1, len(values)):
            chosen = jnp.where(u == index, values[index], chosen)
        return chosen

    def unit(u, _):
        for at, event in events.items():
            pl.when(u == at)(event)
        cross_terms([pick(u, [a for a, _ in units]), pick(u, [b for _, b in units])])
        return 0

    lax.fori_loop(0, len(units), unit, 0)
    send_sums(7 - y, 3)

    out_ref[...] = acc[pl.ds(group_start(w), group)]
    for (way, plane, rank), condition in plan.items():
        pl.when(condition)(halo_copy(way, slot_of[plane][rank]).wait_send)

    def gather(step, _):
        source = lax.rem(w + step, wins)
        pltpu.make_async_remote_copy(
            src_ref=sums_out.at[source],
            dst_ref=sums_in.at[source],
            send_sem=sums_send.at[source],
            recv_sem=sums_recv.at[source],
            device_id={"win": source},
            device_id_type=MESH,
        ).wait_recv()
        out_ref[...] += sums_in[source].astype(jnp.float32).reshape(group, C, LAGS)
        return 0

    lax.fori_loop(1, wins, gather, 0)

    def sent_sums(step, _):
        sums_copy(lax.rem(w + step, wins)).wait_send()
        return 0

    lax.fori_loop(1, wins, sent_sums, 0)


def solution(mesh):
    chans, wins = mesh.shape["chan"], mesh.shape["win"]
    group = BAND // wins

    def local(recordings, channel_live):
        constants = tables(wins * recordings.shape[0])
        operands = (channel_live, recordings, *constants)

        def body(*refs):
            kernel(chans, wins, *refs)

        copies = [pltpu.SMEM(channel_live.shape, channel_live.dtype)]
        copies += [pltpu.VMEM(array.shape, array.dtype) for array in operands[1:]]
        return pl.pallas_call(
            body,
            out_shape=jax.ShapeDtypeStruct((group, C, LAGS), jnp.float32),
            in_specs=[pl.BlockSpec(memory_space=pltpu.HBM)] * len(operands),
            out_specs=pl.BlockSpec(memory_space=pltpu.VMEM),
            scratch_shapes=[
                *copies,
                pltpu.VMEM((SLOTS, 2, K1 * C, K2), jnp.bfloat16),
                pltpu.VMEM((2, K1 * C, 8, K2), jnp.float32),
                pltpu.VMEM((BAND + 16, C, LAGS), jnp.float32),
                pltpu.VMEM((wins, group * C, LAGS), jnp.bfloat16),
                pltpu.VMEM((wins, group * C, LAGS), jnp.bfloat16),
                pltpu.SemaphoreType.DMA((len(operands),)),
                pltpu.SemaphoreType.DMA((4, SLOTS)),
                pltpu.SemaphoreType.DMA((SLOTS,)),
                pltpu.SemaphoreType.DMA((wins,)),
                pltpu.SemaphoreType.DMA((wins,)),
            ],
            compiler_params=pltpu.CompilerParams(
                collective_id=0, has_side_effects=True, vmem_limit_bytes=60 * 1024 * 1024
            ),
            name="correlate",
        )(*operands)

    return jax.shard_map(
        local,
        mesh=mesh,
        in_specs=(P("win", "chan", None), P("chan")),
        out_specs=P("win", "chan", None),
        check_vma=False,
    )
```

```python
import functools
import math

import jax
import jax.numpy as jnp
import numpy as np
from jax import lax
from jax.experimental import pallas as pl
from jax.experimental.pallas import tpu as pltpu
from jax.sharding import PartitionSpec as P

NT = 4096
NF = 2048
WB = 64
BAND = 128
LAGS = 128
C = 8
N1 = 16
N2 = 256
K1 = 16
K2 = 128
PLANE = 4
PLANES = 5
SLOTS = PLANE * PLANES
MESH = pl.DeviceIdType.MESH
SAME, ACROSS = "same", "across"
T1, A1, HERE = "t1", "a1", "here"
ISSUE = [(T1, ACROSS), (T1, SAME), (A1, SAME), (HERE, ACROSS), (A1, ACROSS)]
FAR = "far"
NEAR = [(2, ACROSS), (1, SAME), (1, ACROSS), (3, SAME), (3, ACROSS)]
NEAR_WAITS = [(1, SAME), (2, ACROSS), (1, ACROSS), (3, SAME), (3, ACROSS)]
PLACES = [*NEAR, (0, SAME), (4, SAME), FAR]

def bin_order():
    lane = np.arange(K2)
    return 4 * (lane % 32) + lane // 32


def tables(window_count):
    tau = 2.0 * math.pi
    k1, n1, n2 = np.arange(K1), np.arange(N1), np.arange(N2)
    k2 = bin_order()
    first = tau * (np.outer(k1, n1) % 16) / 16.0
    first = np.concatenate([np.cos(first), -np.sin(first)], axis=0)
    first = np.kron(first, np.eye(C))
    twiddle = tau * (np.outer(k1, n2) % NT) / NT
    twiddle = np.stack([np.cos(twiddle), -np.sin(twiddle)])
    twiddle = np.repeat(twiddle, C, axis=1)
    second = tau * (np.outer(n2, k2) % N2) / N2
    cos, sin = np.cos(second), np.sin(second)
    second = np.stack([np.concatenate([cos, sin]), np.concatenate([-sin, cos])])
    bins = k1[:, None] + K1 * k2[None, :]
    lag = tau * ((bins[:, :, None] * (np.arange(LAGS) - LAGS // 2)) % NT) / NT
    factor = 1.0 / math.sqrt(window_count * NF)
    lag = np.concatenate([np.cos(lag) * factor, -np.sin(lag) * factor], axis=1)
    return (
        jnp.asarray(first, jnp.bfloat16),
        jnp.asarray(twiddle, jnp.float32),
        jnp.asarray(second, jnp.bfloat16),
        jnp.asarray(lag, jnp.bfloat16),
    )


def kernel(
    chans,
    wins,
    live_hbm,
    x_hbm,
    first_hbm,
    twiddle_hbm,
    second_hbm,
    lag_hbm,
    out_ref,
    live_ref,
    x_ref,
    first_ref,
    twiddle_ref,
    second_ref,
    lag_ref,
    halo,
    ownb,
    acc,
    sums_out,
    sums_in,
    fetch_sem,
    halo_send,
    mate_send,
    relay_send,
    halo_recv,
    sums_send,
    sums_recv,
):
    j = lax.axis_index("chan")
    w = lax.axis_index("win")
    group = BAND // wins
    planes = chans // PLANE
    z, r = j // PLANE, j % PLANE
    y, core = r // 2, r % 2
    beside = 2 - 2 * y
    own = 2 * PLANE + r

    fetches = [
        pltpu.make_async_copy(source, target, fetch_sem.at[index])
        for index, (source, target) in enumerate(
            (
                (x_hbm, x_ref),
                (first_hbm, first_ref),
                (twiddle_hbm, twiddle_ref),
                (second_hbm, second_ref),
                (live_hbm, live_ref),
                (lag_hbm, lag_ref),
            )
        )
    ]

    def exists(plane):
        there = z + plane - 2
        return (there >= 0) & (there < planes)

    side, mate = j + 2 - 4 * y, j + 1 - 2 * core
    towards = 2 * y - 1
    always = j >= 0
    has = [exists(plane) for plane in range(PLANES)]
    has_t1, has_a1 = (has[1] & (y == 0)) | (has[3] & (y == 1)), (has[3] & (y == 0)) | (has[1] & (y == 1))
    targets = {
        (T1, SAME): (-towards, j, has_a1),
        (A1, SAME): (towards, j, has_t1),
        (HERE, ACROSS): (0, side, always),
        (T1, ACROSS): (towards, side, has_t1),
        (A1, ACROSS): (-towards, side, has_a1),
    }

    barrier = pltpu.get_barrier_semaphore()

    def greet(there):
        pl.semaphore_signal(barrier, inc=1, device_id=there, device_id_type=MESH)

    greeted = 1 + (wins - 1)
    greet({"chan": mate})
    for up, there, present in targets.values():
        pl.when(present)(lambda: greet({"chan": there + PLANE * up}))
        greeted += present.astype(jnp.int32)
    for fetch in fetches:
        fetch.start()
    for d in range(1, wins):
        greet({"win": lax.rem(w + d, wins)})

    fetches[0].wait()
    fetches[1].wait()
    x = x_ref[0].astype(jnp.float32)
    pieces = jnp.concatenate([x[:, N2 * n1 : N2 * (n1 + 1)] for n1 in range(N1)], axis=0)
    s = jnp.dot(first_ref[...], pieces.astype(jnp.bfloat16), preferred_element_type=jnp.float32)
    s_re, s_im = s[: K1 * C], s[K1 * C :]
    fetches[2].wait()
    fetches[3].wait()
    t_re, t_im = twiddle_ref[0], twiddle_ref[1]
    y_re = (s_re * t_re - s_im * t_im).astype(jnp.bfloat16)
    y_im = (s_re * t_im + s_im * t_re).astype(jnp.bfloat16)
    spec = jnp.dot(
        jnp.concatenate([y_re, y_im], axis=1),
        jnp.concatenate([second_ref[0], second_ref[1]], axis=1),
        preferred_element_type=jnp.float32,
    )
    energy = spec[:, :K2] * spec[:, :K2] + spec[:, K2:] * spec[:, K2:]
    energy = jnp.sum(energy.reshape(K1, C, K2), axis=0)
    energy = energy + pltpu.roll(energy, 64, 1)
    energy = energy + pltpu.roll(energy, 32, 1)
    row = lax.broadcasted_iota(jnp.int32, (C, K2), 0)
    live = jnp.zeros((C, K2), jnp.float32)
    fetches[4].wait()
    for c in range(C):
        live = jnp.where(row == c, live_ref[c].astype(jnp.float32), live)
    factor = (1.0 / jnp.sqrt(energy * (1.0 / WB) + 1e-6)) * live
    factor = jnp.broadcast_to(factor[None], (K1, C, K2)).reshape(K1 * C, K2)
    white_re = (spec[:, :K2] * factor).astype(jnp.bfloat16)
    white_im = (spec[:, K2:] * factor).astype(jnp.bfloat16)
    halo[own, 0] = white_re
    halo[own, 1] = white_im

    pl.semaphore_wait(barrier, greeted)

    far_plane = 2 + 2 * towards
    slot_of = {
        place: PLANE * place[0] + (r if place[1] == SAME else beside + core) for place in PLACES[:-1]
    }
    slot_of[FAR] = PLANE * far_plane + beside + core
    to_mate = mate - j
    arrives = {place: has[place[0]] for place in PLACES[:-1]}
    arrives[FAR] = (has[0] & (y == 0)) | (has[4] & (y == 1))
    passed_on, from_mate = dict(arrives), dict(arrives)
    passed_on[0, SAME] = has[0] & (core == 1)
    from_mate[0, SAME] = has[0] & (core == 0)
    passed_on[4, SAME] = has[4] & (core == 0)
    from_mate[4, SAME] = has[4] & (core == 1)
    pair_of = {place: slot_of[place] + to_mate for place in PLACES}
    pair_of[0, SAME] = slot_of[0, SAME] + jnp.where(core == 0, to_mate, 0)
    pair_of[4, SAME] = slot_of[4, SAME] + jnp.where(core == 1, to_mate, 0)

    def out_copy(place):
        up, there, _ = targets[place]
        return pltpu.make_async_remote_copy(
            src_ref=halo.at[own],
            dst_ref=halo.at[own - PLANE * up],
            send_sem=halo_send.at[ISSUE.index(place)],
            recv_sem=halo_recv.at[own - PLANE * up],
            device_id={"chan": there + PLANE * up},
            device_id_type=MESH,
        )

    inside = has[1] & has[3]
    relays = {
        (1, SAME): (1, inside),
        (3, SAME): (-1, inside),
        (1, ACROSS): (1, inside & (y == 0)),
        (3, ACROSS): (-1, inside & (y == 1)),
    }

    def relay_copy(place):
        up, slot = relays[place][0], slot_of[place]
        return pltpu.make_async_remote_copy(
            src_ref=halo.at[slot],
            dst_ref=halo.at[slot - PLANE * up],
            send_sem=relay_send.at[PLACES.index(place)],
            recv_sem=halo_recv.at[slot - PLANE * up],
            device_id={"chan": j + PLANE * up},
            device_id_type=MESH,
        )

    def mate_copy(slot):
        return pltpu.make_async_remote_copy(
            src_ref=halo.at[slot],
            dst_ref=halo.at[slot],
            send_sem=mate_send.at[slot],
            recv_sem=halo_recv.at[slot],
            device_id={"chan": mate},
            device_id_type=MESH,
        )

    for place in ISSUE:
        pl.when(targets[place][2])(lambda: out_copy(place).start())
    mate_copy(own).start()

    for plane in (0, 1, 3, 4):

        @pl.when(jnp.logical_not(exists(plane)))
        def _():
            def clear(rank, _):
                halo[PLANE * plane + rank] = jnp.zeros((2, K1 * C, K2), jnp.bfloat16)
                return 0

            lax.fori_loop(0, PLANE, clear, 0)

    ownb[0] = jnp.broadcast_to(white_re.astype(jnp.float32)[:, None, :], (K1 * C, 8, K2))
    ownb[1] = jnp.broadcast_to(white_im.astype(jnp.float32)[:, None, :], (K1 * C, 8, K2))
    fetches[5].wait()

    def cross_terms(slots):
        total = jnp.zeros((64 * len(slots), LAGS), jnp.float32)
        for pair in range(K1 // 2):
            rows = slice(16 * pair, 16 * pair + 16)
            blocks = [
                (
                    halo[slot, 0, rows].astype(jnp.float32),
                    halo[slot, 1, rows].astype(jnp.float32),
                )
                for slot in slots
            ]
            for half in (0, 1):
                k1 = 2 * pair + half
                own_re, own_im = ownb[0, C * k1 : C * k1 + C], ownb[1, C * k1 : C * k1 + C]
                parts = []
                for block_re, block_im in blocks:
                    p_re = block_re[8 * half : 8 * half + 8][None]
                    p_im = block_im[8 * half : 8 * half + 8][None]
                    re = own_re * p_re + own_im * p_im
                    im = own_im * p_re - own_re * p_im
                    parts.append(
                        jnp.concatenate([re.reshape(64, K2), im.reshape(64, K2)], axis=1)
                    )
                cross = jnp.concatenate(parts, axis=0).astype(jnp.bfloat16)
                total += jnp.dot(cross, lag_ref[k1], preferred_element_type=jnp.float32)
        for index, slot in enumerate(slots):
            for c in range(C):
                value = total[64 * index + 8 * c : 64 * index + 8 * c + 8]
                acc[pl.ds(8 * (slot - r) + 7 - c, 8), c, :] = value

    def group_start(g):
        return group * g + 7 + (g >= wins // 2).astype(jnp.int32)

    def sums_copy(g):
        return pltpu.make_async_remote_copy(
            src_ref=sums_out.at[g],
            dst_ref=sums_in.at[w],
            send_sem=sums_send.at[g],
            recv_sem=sums_recv.at[w],
            device_id={"win": g},
            device_id_type=MESH,
        )

    def send_sums(first_group, count):
        def one(index, _):
            g = first_group + lax.rem(w + index, count)

            @pl.when(g != w)
            def _():
                value = acc[pl.ds(group_start(g), group)]
                sums_out[g] = value.reshape(group * C, LAGS).astype(jnp.bfloat16)
                sums_copy(g).start()

            return 0

        lax.fori_loop(0, count, one, 0)

    def by_column(first, second):
        return jnp.where(y == 0, first, second)

    def either(conditions, first, second):
        return (conditions[first] & (y == 0)) | (conditions[second] & (y == 1))

    last = [(FAR, (4, SAME)), ((4, SAME), FAR)]
    units = [(own, own + to_mate)] + [(slot_of[place], pair_of[place]) for place in [*NEAR, (0, SAME)]]
    units += [(by_column(slot_of[a], slot_of[b]), by_column(pair_of[a], pair_of[b])) for a, b in last]

    def from_chip(place):
        pl.when(arrives[place])(lambda: mate_copy(slot_of[place]).wait_recv())
        if place in relays:
            pl.when(relays[place][1])(lambda: relay_copy(place).start())
        pl.when(passed_on[place])(lambda: mate_copy(slot_of[place]).start())

    def last_from_chip(index):
        slot = by_column(*(slot_of[place] for place in last[index]))
        pl.when(either(arrives, *last[index]))(lambda: mate_copy(slot).wait_recv())
        pl.when(either(passed_on, *last[index]))(lambda: mate_copy(slot).start())

    def from_core(place):
        pl.when(from_mate[place])(lambda: mate_copy(slot_of[place] + to_mate).wait_recv())

    def last_from_core(index):
        slot = by_column(*(slot_of[place] for place in last[index])) + to_mate
        pl.when(either(from_mate, *last[index]))(lambda: mate_copy(slot).wait_recv())

    def before(u):
        if u == 0:
            mate_copy(own + to_mate).wait_recv()
        elif u <= len(NEAR):
            if u == 1:
                for place in NEAR_WAITS:
                    from_chip(place)
            from_core(NEAR[u - 1])
        elif u == 6:
            from_chip((0, SAME))
            send_sums(2 - y, 5)
            last_from_chip(0)
            from_core((0, SAME))
        elif u == 7:
            send_sums(0, y)
            last_from_chip(1)
            last_from_core(0)
        else:
            send_sums(0, 2 - 2 * y)
            last_from_core(1)

    events = {u: functools.partial(before, u) for u in range(len(units))}

    def pick(u, values):
        chosen = values[0]
        for index in range(1, len(values)):
            chosen = jnp.where(u == index, values[index], chosen)
        return chosen

    def unit(u, _):
        for at, event in events.items():
            pl.when(u == at)(event)
        cross_terms([pick(u, [a for a, _ in units]), pick(u, [b for _, b in units])])
        return 0

    lax.fori_loop(0, len(units), unit, 0)

    send_sums(7 - y, 1 + y)

    out_ref[...] = acc[pl.ds(group_start(w), group)]
    for place in relays:
        pl.when(relays[place][1])(lambda: relay_copy(place).wait_send())
    for place in targets:
        pl.when(targets[place][2])(lambda: out_copy(place).wait_send())
    for place in PLACES:
        pl.when(passed_on[place])(lambda: mate_copy(slot_of[place]).wait_send())
    mate_copy(own).wait_send()

    def gather(step, _):
        source = lax.rem(w + step, wins)
        pltpu.make_async_remote_copy(
            src_ref=sums_out.at[source],
            dst_ref=sums_in.at[source],
            send_sem=sums_send.at[source],
            recv_sem=sums_recv.at[source],
            device_id={"win": source},
            device_id_type=MESH,
        ).wait_recv()
        out_ref[...] += sums_in[source].astype(jnp.float32).reshape(group, C, LAGS)
        return 0

    lax.fori_loop(1, wins, gather, 0)

    def sent_sums(step, _):
        sums_copy(lax.rem(w + step, wins)).wait_send()
        return 0

    lax.fori_loop(1, wins, sent_sums, 0)


def solution(mesh):
    chans, wins = mesh.shape["chan"], mesh.shape["win"]
    group = BAND // wins

    def local(recordings, channel_live):
        constants = tables(wins * recordings.shape[0])
        operands = (channel_live, recordings, *constants)
        operands = [pltpu.with_memory_space_constraint(array, pltpu.HBM) for array in operands]

        def body(*refs):
            kernel(chans, wins, *refs)

        copies = [pltpu.SMEM(channel_live.shape, channel_live.dtype)]
        copies += [pltpu.VMEM(array.shape, array.dtype) for array in operands[1:]]
        return pl.pallas_call(
            body,
            out_shape=pltpu.VMEM((group, C, LAGS), jnp.float32),
            in_specs=[pl.BlockSpec(memory_space=pltpu.HBM)] * len(operands),
            out_specs=pl.BlockSpec(memory_space=pltpu.VMEM),
            scratch_shapes=[
                *copies,
                pltpu.VMEM((SLOTS, 2, K1 * C, K2), jnp.bfloat16),
                pltpu.VMEM((2, K1 * C, 8, K2), jnp.float32),
                pltpu.VMEM((BAND + 16, C, LAGS), jnp.float32),
                pltpu.VMEM((wins, group * C, LAGS), jnp.bfloat16),
                pltpu.VMEM((wins, group * C, LAGS), jnp.bfloat16),
                pltpu.SemaphoreType.DMA((len(operands),)),
                pltpu.SemaphoreType.DMA((8,)),
                pltpu.SemaphoreType.DMA((SLOTS,)),
                pltpu.SemaphoreType.DMA((8,)),
                pltpu.SemaphoreType.DMA((SLOTS,)),
                pltpu.SemaphoreType.DMA((wins,)),
                pltpu.SemaphoreType.DMA((wins,)),
            ],
            compiler_params=pltpu.CompilerParams(
                collective_id=0, has_side_effects=True, vmem_limit_bytes=24 * 1024 * 1024
            ),
            name="correlate",
        )(*operands)

    return jax.shard_map(
        local,
        mesh=mesh,
        in_specs=(P("win", "chan", None), P("chan")),
        out_specs=P("win", "chan", None),
        check_vma=False,
    )
```

```python
import functools
import math

import jax
import jax.numpy as jnp
import numpy as np
from jax import lax
from jax.experimental import pallas as pl
from jax.experimental.pallas import tpu as pltpu
from jax.sharding import PartitionSpec as P

NT = 4096
NF = 2048
WB = 64
BAND = 128
LAGS = 128
C = 8
N1 = 16
N2 = 256
K1 = 16
K2 = 128
PLANE = 4
WIN_X = 4
PLANES = 5
SLOTS = PLANE * PLANES
MESH = pl.DeviceIdType.MESH
SAME, ACROSS = "same", "across"
T1, A1, HERE = "t1", "a1", "here"
ISSUE = [(T1, ACROSS), (T1, SAME), (A1, SAME), (HERE, ACROSS), (A1, ACROSS)]
FAR = "far"
NEAR = [(2, ACROSS), (1, SAME), (1, ACROSS), (3, SAME), (3, ACROSS)]
NEAR_WAITS = [(1, SAME), (2, ACROSS), (1, ACROSS), (3, SAME), (3, ACROSS)]
PLACES = [*NEAR, (0, SAME), (4, SAME), FAR]

def bin_order():
    lane = np.arange(K2)
    return 4 * (lane % 32) + lane // 32


def tables(window_count):
    tau = 2.0 * math.pi
    k1, n1, n2 = np.arange(K1), np.arange(N1), np.arange(N2)
    k2 = bin_order()
    first = tau * (np.outer(k1, n1) % 16) / 16.0
    first = np.concatenate([np.cos(first), -np.sin(first)], axis=0)
    first = np.kron(first, np.eye(C))
    twiddle = tau * (np.outer(k1, n2) % NT) / NT
    twiddle = np.stack([np.cos(twiddle), -np.sin(twiddle)])
    twiddle = np.repeat(twiddle, C, axis=1)
    second = tau * (np.outer(n2, k2) % N2) / N2
    cos, sin = np.cos(second), np.sin(second)
    second = np.stack([np.concatenate([cos, sin]), np.concatenate([-sin, cos])])
    bins = k1[:, None] + K1 * k2[None, :]
    lag = tau * ((bins[:, :, None] * (np.arange(LAGS) - LAGS // 2)) % NT) / NT
    factor = 1.0 / math.sqrt(window_count * NF)
    lag = np.concatenate([np.cos(lag) * factor, -np.sin(lag) * factor], axis=1)
    return (
        jnp.asarray(first, jnp.bfloat16),
        jnp.asarray(twiddle, jnp.float32),
        jnp.asarray(second, jnp.bfloat16),
        jnp.asarray(lag, jnp.bfloat16),
    )


def kernel(
    chans,
    wins,
    live_hbm,
    x_hbm,
    first_hbm,
    twiddle_hbm,
    second_hbm,
    lag_hbm,
    out_ref,
    live_ref,
    x_ref,
    first_ref,
    twiddle_ref,
    second_ref,
    lag_ref,
    halo,
    ownb,
    acc,
    sums_out,
    sums_in,
    fetch_sem,
    halo_send,
    mate_send,
    relay_send,
    halo_recv,
    sums_send,
    sums_recv,
    row_in,
    rest_in,
):
    j = lax.axis_index("chan")
    w = lax.axis_index("win")
    group = BAND // wins
    planes = chans // PLANE
    z, r = j // PLANE, j % PLANE
    y, core = r // 2, r % 2
    beside = 2 - 2 * y
    own = 2 * PLANE + r

    fetches = [
        pltpu.make_async_copy(source, target, fetch_sem.at[index])
        for index, (source, target) in enumerate(
            (
                (x_hbm, x_ref),
                (first_hbm, first_ref),
                (twiddle_hbm, twiddle_ref),
                (second_hbm, second_ref),
                (live_hbm, live_ref),
                (lag_hbm, lag_ref),
            )
        )
    ]

    def exists(plane):
        there = z + plane - 2
        return (there >= 0) & (there < planes)

    side, mate = j + 2 - 4 * y, j + 1 - 2 * core
    towards = 2 * y - 1
    always = j >= 0
    has = [exists(plane) for plane in range(PLANES)]
    has_t1, has_a1 = (has[1] & (y == 0)) | (has[3] & (y == 1)), (has[3] & (y == 0)) | (has[1] & (y == 1))
    targets = {
        (T1, SAME): (-towards, j, has_a1),
        (A1, SAME): (towards, j, has_t1),
        (HERE, ACROSS): (0, side, always),
        (T1, ACROSS): (towards, side, has_t1),
        (A1, ACROSS): (-towards, side, has_a1),
    }

    fetches[0].start()
    fetches[1].start()
    barrier = pltpu.get_barrier_semaphore()

    def greet(there):
        pl.semaphore_signal(barrier, inc=1, device_id=there, device_id_type=MESH)

    row, row_width = w // WIN_X * WIN_X, WIN_X
    beside_x = [row + lax.rem(w + step, row_width) for step in (1, row_width - 1)]
    beyond_y = lax.rem(w + WIN_X, wins)
    greeted = 1 + 3
    greet({"chan": mate})
    for up, there, present in targets.values():
        pl.when(present)(lambda: greet({"chan": there + PLANE * up}))
        greeted += present.astype(jnp.int32)
    for there in (*beside_x, beyond_y):
        greet({"win": there})
    for fetch in fetches[2:]:
        fetch.start()

    fetches[0].wait()
    fetches[1].wait()
    x = x_ref[0].astype(jnp.float32)
    pieces = jnp.concatenate([x[:, N2 * n1 : N2 * (n1 + 1)] for n1 in range(N1)], axis=0)
    s = jnp.dot(first_ref[...], pieces.astype(jnp.bfloat16), preferred_element_type=jnp.float32)
    s_re, s_im = s[: K1 * C], s[K1 * C :]
    fetches[2].wait()
    fetches[3].wait()
    t_re, t_im = twiddle_ref[0], twiddle_ref[1]
    y_re = (s_re * t_re - s_im * t_im).astype(jnp.bfloat16)
    y_im = (s_re * t_im + s_im * t_re).astype(jnp.bfloat16)
    spec = jnp.dot(
        jnp.concatenate([y_re, y_im], axis=1),
        jnp.concatenate([second_ref[0], second_ref[1]], axis=1),
        preferred_element_type=jnp.float32,
    )
    energy = spec[:, :K2] * spec[:, :K2] + spec[:, K2:] * spec[:, K2:]
    energy = jnp.sum(energy.reshape(K1, C, K2), axis=0)
    energy = energy + pltpu.roll(energy, 64, 1)
    energy = energy + pltpu.roll(energy, 32, 1)
    row = lax.broadcasted_iota(jnp.int32, (C, K2), 0)
    live = jnp.zeros((C, K2), jnp.float32)
    fetches[4].wait()
    for c in range(C):
        live = jnp.where(row == c, live_ref[c].astype(jnp.float32), live)
    factor = (1.0 / jnp.sqrt(energy * (1.0 / WB) + 1e-6)) * live
    factor = jnp.broadcast_to(factor[None], (K1, C, K2)).reshape(K1 * C, K2)
    white_re = (spec[:, :K2] * factor).astype(jnp.bfloat16)
    white_im = (spec[:, K2:] * factor).astype(jnp.bfloat16)
    halo[own, 0] = white_re
    halo[own, 1] = white_im

    pl.semaphore_wait(barrier, greeted)

    far_plane = 2 + 2 * towards
    slot_of = {
        place: PLANE * place[0] + (r if place[1] == SAME else beside + core) for place in PLACES[:-1]
    }
    slot_of[FAR] = PLANE * far_plane + beside + core
    to_mate = mate - j
    arrives = {place: has[place[0]] for place in PLACES[:-1]}
    arrives[FAR] = (has[0] & (y == 0)) | (has[4] & (y == 1))
    passed_on, from_mate = dict(arrives), dict(arrives)
    passed_on[0, SAME] = has[0] & (core == 1)
    from_mate[0, SAME] = has[0] & (core == 0)
    passed_on[4, SAME] = has[4] & (core == 0)
    from_mate[4, SAME] = has[4] & (core == 1)
    pair_of = {place: slot_of[place] + to_mate for place in PLACES}
    pair_of[0, SAME] = slot_of[0, SAME] + jnp.where(core == 0, to_mate, 0)
    pair_of[4, SAME] = slot_of[4, SAME] + jnp.where(core == 1, to_mate, 0)

    def out_copy(place):
        up, there, _ = targets[place]
        return pltpu.make_async_remote_copy(
            src_ref=halo.at[own],
            dst_ref=halo.at[own - PLANE * up],
            send_sem=halo_send.at[ISSUE.index(place)],
            recv_sem=halo_recv.at[own - PLANE * up],
            device_id={"chan": there + PLANE * up},
            device_id_type=MESH,
        )

    inside = has[1] & has[3]
    relays = {
        (1, SAME): (1, inside),
        (3, SAME): (-1, inside),
        (1, ACROSS): (1, inside & (y == 0)),
        (3, ACROSS): (-1, inside & (y == 1)),
    }

    def relay_copy(place):
        up, slot = relays[place][0], slot_of[place]
        return pltpu.make_async_remote_copy(
            src_ref=halo.at[slot],
            dst_ref=halo.at[slot - PLANE * up],
            send_sem=relay_send.at[PLACES.index(place)],
            recv_sem=halo_recv.at[slot - PLANE * up],
            device_id={"chan": j + PLANE * up},
            device_id_type=MESH,
        )

    def mate_copy(slot):
        return pltpu.make_async_remote_copy(
            src_ref=halo.at[slot],
            dst_ref=halo.at[slot],
            send_sem=mate_send.at[slot],
            recv_sem=halo_recv.at[slot],
            device_id={"chan": mate},
            device_id_type=MESH,
        )

    for place in ISSUE:
        pl.when(targets[place][2])(lambda: out_copy(place).start())
    mate_copy(own).start()

    def tell(semaphore, there):
        pl.semaphore_signal(semaphore, inc=1, device_id={"win": there}, device_id_type=MESH)

    for there in beside_x:
        tell(row_in, there)

    for plane in (0, 1, 3, 4):

        @pl.when(jnp.logical_not(exists(plane)))
        def _():
            def clear(rank, _):
                halo[PLANE * plane + rank] = jnp.zeros((2, K1 * C, K2), jnp.bfloat16)
                return 0

            lax.fori_loop(0, PLANE, clear, 0)

    ownb[0] = jnp.broadcast_to(white_re.astype(jnp.float32)[:, None, :], (K1 * C, 8, K2))
    ownb[1] = jnp.broadcast_to(white_im.astype(jnp.float32)[:, None, :], (K1 * C, 8, K2))
    fetches[5].wait()

    def cross_terms(slots):
        total = jnp.zeros((64 * len(slots), LAGS), jnp.float32)
        for pair in range(K1 // 2):
            rows = slice(16 * pair, 16 * pair + 16)
            blocks = [
                (
                    halo[slot, 0, rows].astype(jnp.float32),
                    halo[slot, 1, rows].astype(jnp.float32),
                )
                for slot in slots
            ]
            for half in (0, 1):
                k1 = 2 * pair + half
                own_re, own_im = ownb[0, C * k1 : C * k1 + C], ownb[1, C * k1 : C * k1 + C]
                parts = []
                for block_re, block_im in blocks:
                    p_re = block_re[8 * half : 8 * half + 8][None]
                    p_im = block_im[8 * half : 8 * half + 8][None]
                    re = own_re * p_re + own_im * p_im
                    im = own_im * p_re - own_re * p_im
                    parts.append(
                        jnp.concatenate([re.reshape(64, K2), im.reshape(64, K2)], axis=1)
                    )
                cross = jnp.concatenate(parts, axis=0).astype(jnp.bfloat16)
                total += jnp.dot(cross, lag_ref[k1], preferred_element_type=jnp.float32)
        for index, slot in enumerate(slots):
            for c in range(C):
                value = total[64 * index + 8 * c : 64 * index + 8 * c + 8]
                acc[pl.ds(8 * (slot - r) + 7 - c, 8), c, :] = value

    def group_start(g):
        return group * g + 7 + (g >= wins // 2).astype(jnp.int32)

    def sums_copy(g):
        return pltpu.make_async_remote_copy(
            src_ref=sums_out.at[g],
            dst_ref=sums_in.at[w],
            send_sem=sums_send.at[g],
            recv_sem=sums_recv.at[w],
            device_id={"win": g},
            device_id_type=MESH,
        )

    def send_sums(first_group, count):
        def one(index, _):
            g = first_group + lax.rem(w + index, count)

            @pl.when(g != w)
            def _():
                value = acc[pl.ds(group_start(g), group)]
                sums_out[g] = value.reshape(group * C, LAGS).astype(jnp.bfloat16)
                sums_copy(g).start()

            return 0

        lax.fori_loop(0, count, one, 0)

    def by_column(first, second):
        return jnp.where(y == 0, first, second)

    def either(conditions, first, second):
        return (conditions[first] & (y == 0)) | (conditions[second] & (y == 1))

    last = [(FAR, (4, SAME)), ((4, SAME), FAR)]
    units = [(own, own + to_mate)] + [(slot_of[place], pair_of[place]) for place in [*NEAR, (0, SAME)]]
    units += [(by_column(slot_of[a], slot_of[b]), by_column(pair_of[a], pair_of[b])) for a, b in last]

    def from_chip(place):
        pl.when(arrives[place])(lambda: mate_copy(slot_of[place]).wait_recv())
        if place in relays:
            pl.when(relays[place][1])(lambda: relay_copy(place).start())
        pl.when(passed_on[place])(lambda: mate_copy(slot_of[place]).start())

    def last_from_chip(index):
        slot = by_column(*(slot_of[place] for place in last[index]))
        pl.when(either(arrives, *last[index]))(lambda: mate_copy(slot).wait_recv())
        pl.when(either(passed_on, *last[index]))(lambda: mate_copy(slot).start())

    def from_core(place):
        pl.when(from_mate[place])(lambda: mate_copy(slot_of[place] + to_mate).wait_recv())

    def last_from_core(index):
        slot = by_column(*(slot_of[place] for place in last[index])) + to_mate
        pl.when(either(from_mate, *last[index]))(lambda: mate_copy(slot).wait_recv())

    def before(u):
        if u == 0:
            mate_copy(own + to_mate).wait_recv()
        elif u <= len(NEAR):
            if u == 1:
                for place in NEAR_WAITS:
                    from_chip(place)
                pl.semaphore_wait(row_in, 2)
                tell(rest_in, beyond_y)
            from_core(NEAR[u - 1])
        elif u == 6:
            from_chip((0, SAME))
            pl.semaphore_wait(rest_in, 1)
            send_sums(2 - y, 5)
            last_from_chip(0)
            from_core((0, SAME))
        elif u == 7:
            send_sums(0, y)
            last_from_chip(1)
            last_from_core(0)
        else:
            send_sums(0, 2 - 2 * y)
            last_from_core(1)

    events = {u: functools.partial(before, u) for u in range(len(units))}

    def pick(u, values):
        chosen = values[0]
        for index in range(1, len(values)):
            chosen = jnp.where(u == index, values[index], chosen)
        return chosen

    def unit(u, _):
        for at, event in events.items():
            pl.when(u == at)(event)
        cross_terms([pick(u, [a for a, _ in units]), pick(u, [b for _, b in units])])
        return 0

    lax.fori_loop(0, len(units), unit, 0)

    send_sums(7 - y, 1 + y)

    out_ref[...] = acc[pl.ds(group_start(w), group)]
    for place in relays:
        pl.when(relays[place][1])(lambda: relay_copy(place).wait_send())
    for place in targets:
        pl.when(targets[place][2])(lambda: out_copy(place).wait_send())
    for place in PLACES:
        pl.when(passed_on[place])(lambda: mate_copy(slot_of[place]).wait_send())
    mate_copy(own).wait_send()

    def gather(step, _):
        source = lax.rem(w + step, wins)
        pltpu.make_async_remote_copy(
            src_ref=sums_out.at[source],
            dst_ref=sums_in.at[source],
            send_sem=sums_send.at[source],
            recv_sem=sums_recv.at[source],
            device_id={"win": source},
            device_id_type=MESH,
        ).wait_recv()
        out_ref[...] += sums_in[source].astype(jnp.float32).reshape(group, C, LAGS)
        return 0

    lax.fori_loop(1, wins, gather, 0)

    def sent_sums(step, _):
        sums_copy(lax.rem(w + step, wins)).wait_send()
        return 0

    lax.fori_loop(1, wins, sent_sums, 0)


def solution(mesh):
    chans, wins = mesh.shape["chan"], mesh.shape["win"]
    group = BAND // wins

    def local(recordings, channel_live):
        constants = tables(wins * recordings.shape[0])
        operands = (channel_live, recordings, *constants)
        operands = [pltpu.with_memory_space_constraint(array, pltpu.HBM) for array in operands]

        def body(*refs):
            kernel(chans, wins, *refs)

        copies = [pltpu.SMEM(channel_live.shape, channel_live.dtype)]
        copies += [pltpu.VMEM(array.shape, array.dtype) for array in operands[1:]]
        return pl.pallas_call(
            body,
            out_shape=pltpu.VMEM((group, C, LAGS), jnp.float32),
            in_specs=[pl.BlockSpec(memory_space=pltpu.HBM)] * len(operands),
            out_specs=pl.BlockSpec(memory_space=pltpu.VMEM),
            scratch_shapes=[
                *copies,
                pltpu.VMEM((SLOTS, 2, K1 * C, K2), jnp.bfloat16),
                pltpu.VMEM((2, K1 * C, 8, K2), jnp.float32),
                pltpu.VMEM((BAND + 16, C, LAGS), jnp.float32),
                pltpu.VMEM((wins, group * C, LAGS), jnp.bfloat16),
                pltpu.VMEM((wins, group * C, LAGS), jnp.bfloat16),
                pltpu.SemaphoreType.DMA((len(operands),)),
                pltpu.SemaphoreType.DMA((8,)),
                pltpu.SemaphoreType.DMA((SLOTS,)),
                pltpu.SemaphoreType.DMA((8,)),
                pltpu.SemaphoreType.DMA((SLOTS,)),
                pltpu.SemaphoreType.DMA((wins,)),
                pltpu.SemaphoreType.DMA((wins,)),
                pltpu.SemaphoreType.REGULAR,
                pltpu.SemaphoreType.REGULAR,
            ],
            compiler_params=pltpu.CompilerParams(
                collective_id=0, has_side_effects=True, vmem_limit_bytes=24 * 1024 * 1024
            ),
            name="correlate",
        )(*operands)

    return jax.shard_map(
        local,
        mesh=mesh,
        in_specs=(P("win", "chan", None), P("chan")),
        out_specs=P("win", "chan", None),
        check_vma=False,
    )
```

```python
import functools
import math

import jax
import jax.numpy as jnp
import numpy as np
from jax import lax
from jax.experimental import pallas as pl
from jax.experimental.pallas import tpu as pltpu
from jax.sharding import PartitionSpec as P

NT = 4096
NF = 2048
WB = 64
BAND = 128
LAGS = 128
C = 8
N1 = 16
N2 = 256
K1 = 16
K2 = 128
PLANE = 4
WIN_X = 4
PLANES = 5
SLOTS = PLANE * PLANES
MESH = pl.DeviceIdType.MESH
SAME, ACROSS = "same", "across"
T1, A1, HERE = "t1", "a1", "here"
ISSUE = [(T1, SAME), (A1, SAME), (T1, ACROSS), (HERE, ACROSS)]
FAR = "far"
PLACES = [(2, ACROSS), (1, SAME), (1, ACROSS), (3, SAME), (3, ACROSS), (0, SAME), (4, SAME), FAR]

def bin_order():
    lane = np.arange(K2)
    return 4 * (lane % 32) + lane // 32


def tables(window_count):
    tau = 2.0 * math.pi
    k1, n1, n2 = np.arange(K1), np.arange(N1), np.arange(N2)
    k2 = bin_order()
    first = tau * (np.outer(k1, n1) % 16) / 16.0
    first = np.concatenate([np.cos(first), -np.sin(first)], axis=0)
    first = np.kron(first, np.eye(C))
    twiddle = tau * (np.outer(k1, n2) % NT) / NT
    twiddle = np.stack([np.cos(twiddle), -np.sin(twiddle)])
    twiddle = np.repeat(twiddle, C, axis=1)
    second = tau * (np.outer(n2, k2) % N2) / N2
    cos, sin = np.cos(second), np.sin(second)
    second = np.stack([np.concatenate([cos, sin]), np.concatenate([-sin, cos])])
    bins = k1[:, None] + K1 * k2[None, :]
    lag = tau * ((bins[:, :, None] * (np.arange(LAGS) - LAGS // 2)) % NT) / NT
    factor = 1.0 / math.sqrt(window_count * NF)
    lag = np.concatenate([np.cos(lag) * factor, -np.sin(lag) * factor], axis=1)
    return (
        jnp.asarray(first, jnp.bfloat16),
        jnp.asarray(twiddle, jnp.float32),
        jnp.asarray(second, jnp.bfloat16),
        jnp.asarray(lag, jnp.bfloat16),
    )


def kernel(
    chans,
    wins,
    live_hbm,
    x_hbm,
    first_hbm,
    twiddle_hbm,
    second_hbm,
    lag_hbm,
    out_ref,
    live_ref,
    x_ref,
    first_ref,
    twiddle_ref,
    second_ref,
    lag_ref,
    halo,
    ownb,
    acc,
    sums_out,
    sums_in,
    fetch_sem,
    halo_send,
    mate_send,
    relay_send,
    halo_recv,
    sums_send,
    sums_recv,
    row_in,
    rest_in,
):
    j = lax.axis_index("chan")
    w = lax.axis_index("win")
    group = BAND // wins
    planes = chans // PLANE
    z, r = j // PLANE, j % PLANE
    y, core = r // 2, r % 2
    beside = 2 - 2 * y
    own = 2 * PLANE + r

    fetches = [
        pltpu.make_async_copy(source, target, fetch_sem.at[index])
        for index, (source, target) in enumerate(
            (
                (x_hbm, x_ref),
                (first_hbm, first_ref),
                (twiddle_hbm, twiddle_ref),
                (second_hbm, second_ref),
                (live_hbm, live_ref),
                (lag_hbm, lag_ref),
            )
        )
    ]

    def exists(plane):
        there = z + plane - 2
        return (there >= 0) & (there < planes)

    side, mate = j + 2 - 4 * y, j + 1 - 2 * core
    towards = 2 * y - 1
    always = j >= 0
    has = [exists(plane) for plane in range(PLANES)]
    has_t1, has_a1 = (has[1] & (y == 0)) | (has[3] & (y == 1)), (has[3] & (y == 0)) | (has[1] & (y == 1))
    targets = {
        (T1, SAME): (-towards, j, has_a1),
        (A1, SAME): (towards, j, has_t1),
        (HERE, ACROSS): (0, side, always),
        (T1, ACROSS): (towards, side, has_t1),
    }

    fetches[0].start()
    fetches[1].start()
    barrier = pltpu.get_barrier_semaphore()

    def greet(there):
        pl.semaphore_signal(barrier, inc=1, device_id=there, device_id_type=MESH)

    row, row_width = w // WIN_X * WIN_X, WIN_X
    beside_x = [row + lax.rem(w + step, row_width) for step in (1, row_width - 1)]
    beyond_y = lax.rem(w + WIN_X, wins)
    greeted = 1 + 3
    for there in (beyond_y, *beside_x):
        greet({"win": there})
    for up, there, present in targets.values():
        pl.when(present)(lambda: greet({"chan": there + PLANE * up}))
        greeted += present.astype(jnp.int32)
    greet({"chan": mate})
    for fetch in fetches[2:]:
        fetch.start()

    fetches[0].wait()
    fetches[1].wait()
    x = x_ref[0].astype(jnp.float32)
    pieces = jnp.concatenate([x[:, N2 * n1 : N2 * (n1 + 1)] for n1 in range(N1)], axis=0)
    s = jnp.dot(first_ref[...], pieces.astype(jnp.bfloat16), preferred_element_type=jnp.float32)
    s_re, s_im = s[: K1 * C], s[K1 * C :]
    fetches[2].wait()
    fetches[3].wait()
    t_re, t_im = twiddle_ref[0], twiddle_ref[1]
    y_re = (s_re * t_re - s_im * t_im).astype(jnp.bfloat16)
    y_im = (s_re * t_im + s_im * t_re).astype(jnp.bfloat16)
    spec = jnp.dot(
        jnp.concatenate([y_re, y_im], axis=1),
        jnp.concatenate([second_ref[0], second_ref[1]], axis=1),
        preferred_element_type=jnp.float32,
    )
    energy = spec[:, :K2] * spec[:, :K2] + spec[:, K2:] * spec[:, K2:]
    energy = jnp.sum(energy.reshape(K1, C, K2), axis=0)
    energy = energy + pltpu.roll(energy, 64, 1)
    energy = energy + pltpu.roll(energy, 32, 1)
    row = lax.broadcasted_iota(jnp.int32, (C, K2), 0)
    live = jnp.zeros((C, K2), jnp.float32)
    fetches[4].wait()
    for c in range(C):
        live = jnp.where(row == c, live_ref[c].astype(jnp.float32), live)
    factor = (1.0 / jnp.sqrt(energy * (1.0 / WB) + 1e-6)) * live
    factor = jnp.broadcast_to(factor[None], (K1, C, K2)).reshape(K1 * C, K2)
    white_re = (spec[:, :K2] * factor).astype(jnp.bfloat16)
    white_im = (spec[:, K2:] * factor).astype(jnp.bfloat16)
    halo[own, 0] = white_re
    halo[own, 1] = white_im

    pl.semaphore_wait(barrier, greeted)

    far_plane = 2 + 2 * towards
    slot_of = {
        place: PLANE * place[0] + (r if place[1] == SAME else beside + core) for place in PLACES[:-1]
    }
    slot_of[FAR] = PLANE * far_plane + beside + core
    to_mate = mate - j
    arrives = {place: has[place[0]] for place in PLACES[:-1]}
    arrives[FAR] = (has[0] & (y == 0)) | (has[4] & (y == 1))
    passed_on, from_mate = dict(arrives), dict(arrives)
    passed_on[0, SAME] = has[0] & (core == 1)
    from_mate[0, SAME] = has[0] & (core == 0)
    passed_on[4, SAME] = has[4] & (core == 0)
    from_mate[4, SAME] = has[4] & (core == 1)
    pair_of = {place: slot_of[place] + to_mate for place in PLACES}
    pair_of[0, SAME] = slot_of[0, SAME] + jnp.where(core == 0, to_mate, 0)
    pair_of[4, SAME] = slot_of[4, SAME] + jnp.where(core == 1, to_mate, 0)

    def out_copy(place):
        up, there, _ = targets[place]
        return pltpu.make_async_remote_copy(
            src_ref=halo.at[own],
            dst_ref=halo.at[own - PLANE * up],
            send_sem=halo_send.at[ISSUE.index(place)],
            recv_sem=halo_recv.at[own - PLANE * up],
            device_id={"chan": there + PLANE * up},
            device_id_type=MESH,
        )

    inside = has[1] & has[3]
    relays = {
        (1, SAME): (1, inside),
        (3, SAME): (-1, inside),
        (1, ACROSS): (1, inside & (y == 0)),
        (3, ACROSS): (-1, inside & (y == 1)),
        (2, ACROSS): (towards, has_t1),
    }

    def relay_copy(slot, up):
        return pltpu.make_async_remote_copy(
            src_ref=halo.at[slot],
            dst_ref=halo.at[slot - PLANE * up],
            send_sem=relay_send.at[slot],
            recv_sem=halo_recv.at[slot - PLANE * up],
            device_id={"chan": j + PLANE * up},
            device_id_type=MESH,
        )

    def mate_copy(slot):
        return pltpu.make_async_remote_copy(
            src_ref=halo.at[slot],
            dst_ref=halo.at[slot],
            send_sem=mate_send.at[slot],
            recv_sem=halo_recv.at[slot],
            device_id={"chan": mate},
            device_id_type=MESH,
        )

    for place in ISSUE:
        pl.when(targets[place][2])(lambda: out_copy(place).start())
    mate_copy(own).start()

    def tell(semaphore, there):
        pl.semaphore_signal(semaphore, inc=1, device_id={"win": there}, device_id_type=MESH)

    for there in beside_x:
        tell(row_in, there)

    for plane in (0, 1, 3, 4):

        @pl.when(jnp.logical_not(exists(plane)))
        def _():
            def clear(rank, _):
                halo[PLANE * plane + rank] = jnp.zeros((2, K1 * C, K2), jnp.bfloat16)
                return 0

            lax.fori_loop(0, PLANE, clear, 0)

    ownb[0] = jnp.broadcast_to(white_re.astype(jnp.float32)[:, None, :], (K1 * C, 8, K2))
    ownb[1] = jnp.broadcast_to(white_im.astype(jnp.float32)[:, None, :], (K1 * C, 8, K2))
    fetches[5].wait()

    def cross_terms(slots):
        total = jnp.zeros((64 * len(slots), LAGS), jnp.float32)
        for pair in range(K1 // 2):
            rows = slice(16 * pair, 16 * pair + 16)
            blocks = [
                (
                    halo[slot, 0, rows].astype(jnp.float32),
                    halo[slot, 1, rows].astype(jnp.float32),
                )
                for slot in slots
            ]
            for half in (0, 1):
                k1 = 2 * pair + half
                own_re, own_im = ownb[0, C * k1 : C * k1 + C], ownb[1, C * k1 : C * k1 + C]
                parts = []
                for block_re, block_im in blocks:
                    p_re = block_re[8 * half : 8 * half + 8][None]
                    p_im = block_im[8 * half : 8 * half + 8][None]
                    re = own_re * p_re + own_im * p_im
                    im = own_im * p_re - own_re * p_im
                    parts.append(
                        jnp.concatenate([re.reshape(64, K2), im.reshape(64, K2)], axis=1)
                    )
                cross = jnp.concatenate(parts, axis=0).astype(jnp.bfloat16)
                total += jnp.dot(cross, lag_ref[k1], preferred_element_type=jnp.float32)
        for index, slot in enumerate(slots):
            for c in range(C):
                value = total[64 * index + 8 * c : 64 * index + 8 * c + 8]
                acc[pl.ds(8 * (slot - r) + 7 - c, 8), c, :] = value

    def group_start(g):
        return group * g + 7 + (g >= wins // 2).astype(jnp.int32)

    def sums_copy(g):
        return pltpu.make_async_remote_copy(
            src_ref=sums_out.at[g],
            dst_ref=sums_in.at[w],
            send_sem=sums_send.at[g],
            recv_sem=sums_recv.at[w],
            device_id={"win": g},
            device_id_type=MESH,
        )

    def send_sums(first_group, count):
        def one(index, _):
            g = first_group + lax.rem(w + index, count)

            @pl.when(g != w)
            def _():
                value = acc[pl.ds(group_start(g), group)]
                sums_out[g] = value.reshape(group * C, LAGS).astype(jnp.bfloat16)
                sums_copy(g).start()

            return 0

        lax.fori_loop(0, count, one, 0)

    def from_chip(place):
        pl.when(arrives[place])(lambda: mate_copy(slot_of[place]).wait_recv())
        if place in relays:
            pl.when(relays[place][1])(lambda: relay_copy(slot_of[place], relays[place][0]).start())
        pl.when(passed_on[place])(lambda: mate_copy(slot_of[place]).start())

    def from_core(place):
        pl.when(from_mate[place])(lambda: mate_copy(slot_of[place] + to_mate).wait_recv())

    def rest_is_in():
        pl.semaphore_wait(rest_in, 1)

    def row_is_in():
        pl.semaphore_wait(row_in, 2)
        tell(rest_in, beyond_y)

    chip, core_of, sums = (
        lambda *places: [functools.partial(from_chip, place) for place in places],
        lambda place: [functools.partial(from_core, place)],
        lambda first, count: [functools.partial(send_sums, first, count)],
    )
    steps = (
        [(2, ACROSS), (1, SAME), (1, ACROSS), (3, SAME), (0, SAME), FAR, (3, ACROSS), (4, SAME)],
        [(2, ACROSS), (3, SAME), (3, ACROSS), (1, SAME), (1, ACROSS), (0, SAME), (4, SAME), FAR],
    )
    before = (
        {
            1: [row_is_in, *chip((1, SAME), (2, ACROSS), (1, ACROSS), (3, SAME))],
            4: [rest_is_in, *sums(2, 3)],
            5: [*chip((0, SAME)), *sums(5, 1)],
            6: chip(FAR, (3, ACROSS)),
            7: [*sums(0, 2), *chip((4, SAME))],
            8: sums(6, 1),
        },
        {
            1: [row_is_in, *chip((3, SAME), (2, ACROSS), (3, ACROSS), (1, SAME))],
            4: [*chip((1, ACROSS)), rest_is_in, *sums(3, 3)],
            6: [*chip((0, SAME)), *sums(1, 2), *chip((4, SAME))],
            7: [*sums(0, 1), *chip(FAR)],
        },
    )

    def event(u, column):
        if u == 0:
            mate_copy(own + to_mate).wait_recv()
        else:
            for act in [*before[column].get(u, []), *core_of(steps[column][u - 1])]:
                act()

    def before_step(u):
        for column in (0, 1):
            pl.when(y == column)(functools.partial(event, u, column))

    units = [(own, own + to_mate)]
    units += [
        tuple(jnp.where(y == 0, table[a], table[b]) for table in (slot_of, pair_of))
        for a, b in zip(*steps, strict=True)
    ]
    events = {u: functools.partial(before_step, u) for u in range(len(units))}

    def pick(u, values):
        chosen = values[0]
        for index in range(1, len(values)):
            chosen = jnp.where(u == index, values[index], chosen)
        return chosen

    def unit(u, _):
        for at, event in events.items():
            pl.when(u == at)(event)
        cross_terms([pick(u, [a for a, _ in units]), pick(u, [b for _, b in units])])
        return 0

    lax.fori_loop(0, len(units), unit, 0)

    send_sums(7 - y, 1 + y)

    out_ref[...] = acc[pl.ds(group_start(w), group)]
    for place in relays:
        pl.when(relays[place][1])(lambda: relay_copy(slot_of[place], relays[place][0]).wait_send())
    for place in targets:
        pl.when(targets[place][2])(lambda: out_copy(place).wait_send())
    for place in PLACES:
        pl.when(passed_on[place])(lambda: mate_copy(slot_of[place]).wait_send())
    mate_copy(own).wait_send()

    def gather(step, _):
        source = lax.rem(w + step, wins)
        pltpu.make_async_remote_copy(
            src_ref=sums_out.at[source],
            dst_ref=sums_in.at[source],
            send_sem=sums_send.at[source],
            recv_sem=sums_recv.at[source],
            device_id={"win": source},
            device_id_type=MESH,
        ).wait_recv()
        out_ref[...] += sums_in[source].astype(jnp.float32).reshape(group, C, LAGS)
        return 0

    lax.fori_loop(1, wins, gather, 0)

    def sent_sums(step, _):
        sums_copy(lax.rem(w + step, wins)).wait_send()
        return 0

    lax.fori_loop(1, wins, sent_sums, 0)


def solution(mesh):
    chans, wins = mesh.shape["chan"], mesh.shape["win"]
    group = BAND // wins

    def local(recordings, channel_live):
        constants = tables(wins * recordings.shape[0])
        operands = (channel_live, recordings, *constants)
        operands = [pltpu.with_memory_space_constraint(array, pltpu.HBM) for array in operands]

        def body(*refs):
            kernel(chans, wins, *refs)

        copies = [pltpu.SMEM(channel_live.shape, channel_live.dtype)]
        copies += [pltpu.VMEM(array.shape, array.dtype) for array in operands[1:]]
        return pl.pallas_call(
            body,
            out_shape=pltpu.VMEM((group, C, LAGS), jnp.float32),
            in_specs=[pl.BlockSpec(memory_space=pltpu.HBM)] * len(operands),
            out_specs=pl.BlockSpec(memory_space=pltpu.VMEM),
            scratch_shapes=[
                *copies,
                pltpu.VMEM((SLOTS, 2, K1 * C, K2), jnp.bfloat16),
                pltpu.VMEM((2, K1 * C, 8, K2), jnp.float32),
                pltpu.VMEM((BAND + 16, C, LAGS), jnp.float32),
                pltpu.VMEM((wins, group * C, LAGS), jnp.bfloat16),
                pltpu.VMEM((wins, group * C, LAGS), jnp.bfloat16),
                pltpu.SemaphoreType.DMA((len(operands),)),
                pltpu.SemaphoreType.DMA((8,)),
                pltpu.SemaphoreType.DMA((SLOTS,)),
                pltpu.SemaphoreType.DMA((SLOTS,)),
                pltpu.SemaphoreType.DMA((SLOTS,)),
                pltpu.SemaphoreType.DMA((wins,)),
                pltpu.SemaphoreType.DMA((wins,)),
                pltpu.SemaphoreType.REGULAR,
                pltpu.SemaphoreType.REGULAR,
            ],
            compiler_params=pltpu.CompilerParams(
                collective_id=0, has_side_effects=True, vmem_limit_bytes=24 * 1024 * 1024
            ),
            name="correlate",
        )(*operands)

    return jax.shard_map(
        local,
        mesh=mesh,
        in_specs=(P("win", "chan", None), P("chan")),
        out_specs=P("win", "chan", None),
        check_vma=False,
    )
```

```python
import functools
import math

import jax
import jax.numpy as jnp
import numpy as np
from jax import lax
from jax.experimental import pallas as pl
from jax.experimental.pallas import tpu as pltpu
from jax.sharding import PartitionSpec as P

NT = 4096
NF = 2048
WB = 64
BAND = 128
LAGS = 128
C = 8
N1 = 16
N2 = 256
K1 = 16
K2 = 128
PLANE = 4
WIN_X = 4
PLANES = 5
SLOTS = PLANE * PLANES
MESH = pl.DeviceIdType.MESH
SAME, ACROSS = "same", "across"
T1, A1, HERE = "t1", "a1", "here"
ISSUE = [(T1, ACROSS), (T1, SAME), (A1, SAME), (HERE, ACROSS)]
FAR = "far"
PLACES = [(2, ACROSS), (1, SAME), (1, ACROSS), (3, SAME), (3, ACROSS), (0, SAME), (4, SAME), FAR]

def bin_order():
    lane = np.arange(K2)
    return 4 * (lane % 32) + lane // 32


def tables(window_count):
    tau = 2.0 * math.pi
    k1, n1, n2 = np.arange(K1), np.arange(N1), np.arange(N2)
    k2 = bin_order()
    first = tau * (np.outer(k1, n1) % 16) / 16.0
    first = np.concatenate([np.cos(first), -np.sin(first)], axis=0)
    first = np.kron(first, np.eye(C))
    twiddle = tau * (np.outer(k1, n2) % NT) / NT
    twiddle = np.stack([np.cos(twiddle), -np.sin(twiddle)])
    twiddle = np.repeat(twiddle, C, axis=1)
    second = tau * (np.outer(n2, k2) % N2) / N2
    cos, sin = np.cos(second), np.sin(second)
    second = np.stack([np.concatenate([cos, sin]), np.concatenate([-sin, cos])])
    bins = k1[:, None] + K1 * k2[None, :]
    lag = tau * ((bins[:, :, None] * (np.arange(LAGS) - LAGS // 2)) % NT) / NT
    factor = 1.0 / math.sqrt(window_count * NF)
    lag = np.concatenate([np.cos(lag) * factor, -np.sin(lag) * factor], axis=1)
    return (
        jnp.asarray(first, jnp.bfloat16),
        jnp.asarray(twiddle, jnp.float32),
        jnp.asarray(second, jnp.bfloat16),
        jnp.asarray(lag, jnp.bfloat16),
    )


def kernel(
    chans,
    wins,
    live_hbm,
    x_hbm,
    first_hbm,
    twiddle_hbm,
    second_hbm,
    lag_hbm,
    out_ref,
    live_ref,
    x_ref,
    first_ref,
    twiddle_ref,
    second_ref,
    lag_ref,
    halo,
    ownb,
    acc,
    sums_out,
    sums_in,
    fetch_sem,
    halo_send,
    mate_send,
    relay_send,
    halo_recv,
    sums_send,
    sums_recv,
    row_in,
    rest_in,
):
    j = lax.axis_index("chan")
    w = lax.axis_index("win")
    group = BAND // wins
    planes = chans // PLANE
    z, r = j // PLANE, j % PLANE
    y, core = r // 2, r % 2
    beside = 2 - 2 * y
    own = 2 * PLANE + r

    fetches = [
        pltpu.make_async_copy(source, target, fetch_sem.at[index])
        for index, (source, target) in enumerate(
            (
                (x_hbm, x_ref),
                (first_hbm, first_ref),
                (twiddle_hbm, twiddle_ref),
                (second_hbm, second_ref),
                (live_hbm, live_ref),
                (lag_hbm, lag_ref),
            )
        )
    ]

    def exists(plane):
        there = z + plane - 2
        return (there >= 0) & (there < planes)

    side, mate = j + 2 - 4 * y, j + 1 - 2 * core
    towards = 2 * y - 1
    always = j >= 0
    has = [exists(plane) for plane in range(PLANES)]
    has_t1, has_a1 = (has[1] & (y == 0)) | (has[3] & (y == 1)), (has[3] & (y == 0)) | (has[1] & (y == 1))
    targets = {
        (T1, ACROSS): (towards, side, has_t1),
        (T1, SAME): (-towards, j, has_a1),
        (A1, SAME): (towards, j, has_t1),
        (HERE, ACROSS): (0, side, always),
    }

    fetches[0].start()
    fetches[1].start()
    barrier = pltpu.get_barrier_semaphore()

    def greet(there):
        pl.semaphore_signal(barrier, inc=1, device_id=there, device_id_type=MESH)

    row, row_width = w // WIN_X * WIN_X, WIN_X
    beside_x = [row + lax.rem(w + step, row_width) for step in (1, row_width - 1)]
    beyond_y = lax.rem(w + WIN_X, wins)
    greeted = 1 + 3
    for up, there, present in targets.values():
        pl.when(present)(lambda: greet({"chan": there + PLANE * up}))
        greeted += present.astype(jnp.int32)
    for there in (beyond_y, *beside_x):
        greet({"win": there})
    greet({"chan": mate})
    for fetch in fetches[2:]:
        fetch.start()

    fetches[0].wait()
    fetches[1].wait()
    x = x_ref[0].astype(jnp.float32)
    pieces = jnp.concatenate([x[:, N2 * n1 : N2 * (n1 + 1)] for n1 in range(N1)], axis=0)
    s = jnp.dot(first_ref[...], pieces.astype(jnp.bfloat16), preferred_element_type=jnp.float32)
    s_re, s_im = s[: K1 * C], s[K1 * C :]
    fetches[2].wait()
    fetches[3].wait()
    t_re, t_im = twiddle_ref[0], twiddle_ref[1]
    y_re = (s_re * t_re - s_im * t_im).astype(jnp.bfloat16)
    y_im = (s_re * t_im + s_im * t_re).astype(jnp.bfloat16)
    spec = jnp.dot(
        jnp.concatenate([y_re, y_im], axis=1),
        jnp.concatenate([second_ref[0], second_ref[1]], axis=1),
        preferred_element_type=jnp.float32,
    )
    energy = spec[:, :K2] * spec[:, :K2] + spec[:, K2:] * spec[:, K2:]
    energy = jnp.sum(energy.reshape(K1, C, K2), axis=0)
    energy = energy + pltpu.roll(energy, 64, 1)
    energy = energy + pltpu.roll(energy, 32, 1)
    row = lax.broadcasted_iota(jnp.int32, (C, K2), 0)
    live = jnp.zeros((C, K2), jnp.float32)
    fetches[4].wait()
    for c in range(C):
        live = jnp.where(row == c, live_ref[c].astype(jnp.float32), live)
    factor = (1.0 / jnp.sqrt(energy * (1.0 / WB) + 1e-6)) * live
    factor = jnp.broadcast_to(factor[None], (K1, C, K2)).reshape(K1 * C, K2)
    white_re = (spec[:, :K2] * factor).astype(jnp.bfloat16)
    white_im = (spec[:, K2:] * factor).astype(jnp.bfloat16)
    halo[own, 0] = white_re
    halo[own, 1] = white_im

    pl.semaphore_wait(barrier, greeted)

    far_plane = 2 + 2 * towards
    slot_of = {
        place: PLANE * place[0] + (r if place[1] == SAME else beside + core) for place in PLACES[:-1]
    }
    slot_of[FAR] = PLANE * far_plane + beside + core
    to_mate = mate - j
    arrives = {place: has[place[0]] for place in PLACES[:-1]}
    arrives[FAR] = (has[0] & (y == 0)) | (has[4] & (y == 1))
    passed_on, from_mate = dict(arrives), dict(arrives)
    passed_on[0, SAME] = has[0] & (core == 1)
    from_mate[0, SAME] = has[0] & (core == 0)
    passed_on[4, SAME] = has[4] & (core == 0)
    from_mate[4, SAME] = has[4] & (core == 1)
    pair_of = {place: slot_of[place] + to_mate for place in PLACES}
    pair_of[0, SAME] = slot_of[0, SAME] + jnp.where(core == 0, to_mate, 0)
    pair_of[4, SAME] = slot_of[4, SAME] + jnp.where(core == 1, to_mate, 0)

    def out_copy(place):
        up, there, _ = targets[place]
        return pltpu.make_async_remote_copy(
            src_ref=halo.at[own],
            dst_ref=halo.at[own - PLANE * up],
            send_sem=halo_send.at[ISSUE.index(place)],
            recv_sem=halo_recv.at[own - PLANE * up],
            device_id={"chan": there + PLANE * up},
            device_id_type=MESH,
        )

    inside = has[1] & has[3]
    relays = {
        (1, SAME): (1, inside),
        (3, SAME): (-1, inside),
        (1, ACROSS): (1, inside & (y == 0)),
        (3, ACROSS): (-1, inside & (y == 1)),
        (2, ACROSS): (towards, has_t1),
    }

    def relay_copy(slot, up):
        return pltpu.make_async_remote_copy(
            src_ref=halo.at[slot],
            dst_ref=halo.at[slot - PLANE * up],
            send_sem=relay_send.at[slot],
            recv_sem=halo_recv.at[slot - PLANE * up],
            device_id={"chan": j + PLANE * up},
            device_id_type=MESH,
        )

    def mate_copy(slot):
        return pltpu.make_async_remote_copy(
            src_ref=halo.at[slot],
            dst_ref=halo.at[slot],
            send_sem=mate_send.at[slot],
            recv_sem=halo_recv.at[slot],
            device_id={"chan": mate},
            device_id_type=MESH,
        )

    for place in ISSUE:
        pl.when(targets[place][2])(lambda: out_copy(place).start())
    mate_copy(own).start()

    def tell(semaphore, there):
        pl.semaphore_signal(semaphore, inc=1, device_id={"win": there}, device_id_type=MESH)

    for there in beside_x:
        tell(row_in, there)

    for plane in (0, 1, 3, 4):

        @pl.when(jnp.logical_not(exists(plane)))
        def _():
            def clear(rank, _):
                halo[PLANE * plane + rank] = jnp.zeros((2, K1 * C, K2), jnp.bfloat16)
                return 0

            lax.fori_loop(0, PLANE, clear, 0)

    ownb[0] = jnp.broadcast_to(white_re.astype(jnp.float32)[:, None, :], (K1 * C, 8, K2))
    ownb[1] = jnp.broadcast_to(white_im.astype(jnp.float32)[:, None, :], (K1 * C, 8, K2))
    fetches[5].wait()

    def cross_terms(slots):
        total = jnp.zeros((64 * len(slots), LAGS), jnp.float32)
        for pair in range(K1 // 2):
            rows = slice(16 * pair, 16 * pair + 16)
            blocks = [
                (
                    halo[slot, 0, rows].astype(jnp.float32),
                    halo[slot, 1, rows].astype(jnp.float32),
                )
                for slot in slots
            ]
            for half in (0, 1):
                k1 = 2 * pair + half
                own_re, own_im = ownb[0, C * k1 : C * k1 + C], ownb[1, C * k1 : C * k1 + C]
                parts = []
                for block_re, block_im in blocks:
                    p_re = block_re[8 * half : 8 * half + 8][None]
                    p_im = block_im[8 * half : 8 * half + 8][None]
                    re = own_re * p_re + own_im * p_im
                    im = own_im * p_re - own_re * p_im
                    parts.append(
                        jnp.concatenate([re.reshape(64, K2), im.reshape(64, K2)], axis=1)
                    )
                cross = jnp.concatenate(parts, axis=0).astype(jnp.bfloat16)
                total += jnp.dot(cross, lag_ref[k1], preferred_element_type=jnp.float32)
        for index, slot in enumerate(slots):
            for c in range(C):
                value = total[64 * index + 8 * c : 64 * index + 8 * c + 8]
                acc[pl.ds(8 * (slot - r) + 7 - c, 8), c, :] = value

    def group_start(g):
        return group * g + 7 + (g >= wins // 2).astype(jnp.int32)

    def sums_copy(g):
        return pltpu.make_async_remote_copy(
            src_ref=sums_out.at[g],
            dst_ref=sums_in.at[w],
            send_sem=sums_send.at[g],
            recv_sem=sums_recv.at[w],
            device_id={"win": g},
            device_id_type=MESH,
        )

    def send_sums(first_group, count, turned=True):
        def one(index, _):
            g = first_group + (lax.rem(w + index, count) if turned else index)

            @pl.when(g != w)
            def _():
                value = acc[pl.ds(group_start(g), group)]
                sums_out[g] = value.reshape(group * C, LAGS).astype(jnp.bfloat16)
                sums_copy(g).start()

            return 0

        lax.fori_loop(0, count, one, 0)

    def from_chip(place):
        pl.when(arrives[place])(lambda: mate_copy(slot_of[place]).wait_recv())
        if place in relays:
            pl.when(relays[place][1])(lambda: relay_copy(slot_of[place], relays[place][0]).start())
        pl.when(passed_on[place])(lambda: mate_copy(slot_of[place]).start())

    def from_core(place):
        pl.when(from_mate[place])(lambda: mate_copy(slot_of[place] + to_mate).wait_recv())

    def rest_is_in():
        pl.semaphore_wait(rest_in, 1)

    def row_is_in():
        pl.semaphore_wait(row_in, 2)
        tell(rest_in, beyond_y)

    chip, core_of, sums = (
        lambda *places: [functools.partial(from_chip, place) for place in places],
        lambda place: [functools.partial(from_core, place)],
        lambda first, count: [functools.partial(send_sums, first, count)],
    )
    steps = (
        [(2, ACROSS), (1, SAME), (1, ACROSS), (3, SAME), (0, SAME), FAR, (3, ACROSS), (4, SAME)],
        [(2, ACROSS), (3, SAME), (3, ACROSS), (1, SAME), (1, ACROSS), (0, SAME), (4, SAME), FAR],
    )
    before = (
        {
            1: [row_is_in, *chip((1, SAME), (2, ACROSS), (1, ACROSS), (3, SAME))],
            4: [rest_is_in, *sums(2, 3)],
            5: [*chip((0, SAME)), *sums(5, 1)],
            6: chip(FAR, (3, ACROSS)),
            7: [functools.partial(send_sums, 0, 2, turned=False), *chip((4, SAME))],
            8: sums(6, 1),
        },
        {
            1: [row_is_in, *chip((3, SAME), (2, ACROSS), (3, ACROSS), (1, SAME))],
            4: [*chip((1, ACROSS)), rest_is_in, *sums(3, 3)],
            6: [*chip((0, SAME)), *sums(1, 2), *chip((4, SAME))],
            7: [*sums(0, 1), *chip(FAR)],
        },
    )

    def event(u, column):
        if u == 0:
            mate_copy(own + to_mate).wait_recv()
        else:
            for act in [*before[column].get(u, []), *core_of(steps[column][u - 1])]:
                act()

    def before_step(u):
        for column in (0, 1):
            pl.when(y == column)(functools.partial(event, u, column))

    units = [(own, own + to_mate)]
    units += [
        tuple(jnp.where(y == 0, table[a], table[b]) for table in (slot_of, pair_of))
        for a, b in zip(*steps, strict=True)
    ]
    events = {u: functools.partial(before_step, u) for u in range(len(units))}

    def pick(u, values):
        chosen = values[0]
        for index in range(1, len(values)):
            chosen = jnp.where(u == index, values[index], chosen)
        return chosen

    def unit(u, _):
        for at, event in events.items():
            pl.when(u == at)(event)
        cross_terms([pick(u, [a for a, _ in units]), pick(u, [b for _, b in units])])
        return 0

    lax.fori_loop(0, len(units), unit, 0)

    send_sums(7, 1)
    send_sums(6, y)

    out_ref[...] = acc[pl.ds(group_start(w), group)]
    for place in relays:
        pl.when(relays[place][1])(lambda: relay_copy(slot_of[place], relays[place][0]).wait_send())
    for place in targets:
        pl.when(targets[place][2])(lambda: out_copy(place).wait_send())
    for place in PLACES:
        pl.when(passed_on[place])(lambda: mate_copy(slot_of[place]).wait_send())
    mate_copy(own).wait_send()

    def sent_sums(step, _):
        sums_copy(lax.rem(w + step, wins)).wait_send()
        return 0

    lax.fori_loop(1, wins, sent_sums, 0)

    def gather(step, _):
        source = lax.rem(w + step, wins)
        pltpu.make_async_remote_copy(
            src_ref=sums_out.at[source],
            dst_ref=sums_in.at[source],
            send_sem=sums_send.at[source],
            recv_sem=sums_recv.at[source],
            device_id={"win": source},
            device_id_type=MESH,
        ).wait_recv()
        out_ref[...] += sums_in[source].astype(jnp.float32).reshape(group, C, LAGS)
        return 0

    lax.fori_loop(1, wins, gather, 0)


def solution(mesh):
    chans, wins = mesh.shape["chan"], mesh.shape["win"]
    group = BAND // wins

    def local(recordings, channel_live):
        constants = tables(wins * recordings.shape[0])
        operands = (channel_live, recordings, *constants)
        operands = [pltpu.with_memory_space_constraint(array, pltpu.HBM) for array in operands]

        def body(*refs):
            kernel(chans, wins, *refs)

        copies = [pltpu.SMEM(channel_live.shape, channel_live.dtype)]
        copies += [pltpu.VMEM(array.shape, array.dtype) for array in operands[1:]]
        return pl.pallas_call(
            body,
            out_shape=pltpu.VMEM((group, C, LAGS), jnp.float32),
            in_specs=[pl.BlockSpec(memory_space=pltpu.HBM)] * len(operands),
            out_specs=pl.BlockSpec(memory_space=pltpu.VMEM),
            scratch_shapes=[
                *copies,
                pltpu.VMEM((SLOTS, 2, K1 * C, K2), jnp.bfloat16),
                pltpu.VMEM((2, K1 * C, 8, K2), jnp.float32),
                pltpu.VMEM((BAND + 16, C, LAGS), jnp.float32),
                pltpu.VMEM((wins, group * C, LAGS), jnp.bfloat16),
                pltpu.VMEM((wins, group * C, LAGS), jnp.bfloat16),
                pltpu.SemaphoreType.DMA((len(operands),)),
                pltpu.SemaphoreType.DMA((8,)),
                pltpu.SemaphoreType.DMA((SLOTS,)),
                pltpu.SemaphoreType.DMA((SLOTS,)),
                pltpu.SemaphoreType.DMA((SLOTS,)),
                pltpu.SemaphoreType.DMA((wins,)),
                pltpu.SemaphoreType.DMA((wins,)),
                pltpu.SemaphoreType.REGULAR,
                pltpu.SemaphoreType.REGULAR,
            ],
            compiler_params=pltpu.CompilerParams(
                collective_id=0, has_side_effects=True, vmem_limit_bytes=24 * 1024 * 1024
            ),
            name="correlate",
        )(*operands)

    return jax.shard_map(
        local,
        mesh=mesh,
        in_specs=(P("win", "chan", None), P("chan")),
        out_specs=P("win", "chan", None),
        check_vma=False,
    )
```

```python
import functools
import math

import jax
import jax.numpy as jnp
import numpy as np
from jax import lax
from jax.experimental import pallas as pl
from jax.experimental.pallas import tpu as pltpu
from jax.sharding import PartitionSpec as P

NT = 4096
NF = 2048
WB = 64
BAND = 128
LAGS = 128
C = 8
N1 = 16
N2 = 256
K1 = 16
K2 = 128
PLANE = 4
WIN_X = 4
PLANES = 5
SLOTS = PLANE * PLANES
MESH = pl.DeviceIdType.MESH
SAME, ACROSS = "same", "across"
T1, A1, HERE = "t1", "a1", "here"
ISSUE = [(T1, ACROSS), (T1, SAME), (A1, SAME), (HERE, ACROSS)]
FAR = "far"
PLACES = [(2, ACROSS), (1, SAME), (1, ACROSS), (3, SAME), (3, ACROSS), (0, SAME), (4, SAME), FAR]

def bin_order():
    lane = np.arange(K2)
    return 4 * (lane % 32) + lane // 32


def tables(window_count):
    tau = 2.0 * math.pi
    k1, n1, n2 = np.arange(K1), np.arange(N1), np.arange(N2)
    k2 = bin_order()
    first = tau * (np.outer(k1, n1) % 16) / 16.0
    first = np.concatenate([np.cos(first), -np.sin(first)], axis=0)
    first = np.kron(first, np.eye(C))
    twiddle = tau * (np.outer(k1, n2) % NT) / NT
    twiddle = np.stack([np.cos(twiddle), -np.sin(twiddle)])
    twiddle = np.repeat(twiddle, C, axis=1)
    second = tau * (np.outer(n2, k2) % N2) / N2
    cos, sin = np.cos(second), np.sin(second)
    second = np.stack([np.concatenate([cos, sin]), np.concatenate([-sin, cos])])
    bins = k1[:, None] + K1 * k2[None, :]
    lag = tau * ((bins[:, :, None] * (np.arange(LAGS) - LAGS // 2)) % NT) / NT
    factor = 1.0 / math.sqrt(window_count * NF)
    lag = np.concatenate([np.cos(lag) * factor, -np.sin(lag) * factor], axis=1)
    return (
        jnp.asarray(first, jnp.bfloat16),
        jnp.asarray(twiddle, jnp.float32),
        jnp.asarray(second, jnp.bfloat16),
        jnp.asarray(lag, jnp.bfloat16),
    )


def kernel(
    chans,
    wins,
    live_hbm,
    x_hbm,
    first_hbm,
    twiddle_hbm,
    second_hbm,
    lag_hbm,
    out_ref,
    live_ref,
    x_ref,
    first_ref,
    twiddle_ref,
    second_ref,
    lag_ref,
    halo,
    ownb,
    acc,
    sums_out,
    sums_in,
    fetch_sem,
    halo_send,
    mate_send,
    relay_send,
    halo_recv,
    sums_send,
    sums_recv,
    row_in,
    rest_in,
):
    j = lax.axis_index("chan")
    w = lax.axis_index("win")
    group = BAND // wins
    planes = chans // PLANE
    z, r = j // PLANE, j % PLANE
    y, core = r // 2, r % 2
    beside = 2 - 2 * y
    own = 2 * PLANE + r

    fetches = [
        pltpu.make_async_copy(source, target, fetch_sem.at[index])
        for index, (source, target) in enumerate(
            (
                (x_hbm, x_ref),
                (first_hbm, first_ref),
                (twiddle_hbm, twiddle_ref),
                (second_hbm, second_ref),
                (live_hbm, live_ref),
                (lag_hbm, lag_ref),
            )
        )
    ]

    def exists(plane):
        there = z + plane - 2
        return (there >= 0) & (there < planes)

    side, mate = j + 2 - 4 * y, j + 1 - 2 * core
    towards = 2 * y - 1
    always = j >= 0
    has = [exists(plane) for plane in range(PLANES)]
    has_t1, has_a1 = (has[1] & (y == 0)) | (has[3] & (y == 1)), (has[3] & (y == 0)) | (has[1] & (y == 1))
    targets = {
        (T1, ACROSS): (towards, side, has_t1),
        (T1, SAME): (-towards, j, has_a1),
        (A1, SAME): (towards, j, has_t1),
        (HERE, ACROSS): (0, side, always),
    }

    fetches[0].start()
    fetches[1].start()
    barrier = pltpu.get_barrier_semaphore()

    def greet(there):
        pl.semaphore_signal(barrier, inc=1, device_id=there, device_id_type=MESH)

    row, row_width = w // WIN_X * WIN_X, WIN_X
    beside_x = [row + lax.rem(w + step, row_width) for step in (1, row_width - 1)]
    beyond_y = lax.rem(w + WIN_X, wins)
    greeted = 1 + 3
    for up, there, present in targets.values():
        pl.when(present)(lambda: greet({"chan": there + PLANE * up}))
        greeted += present.astype(jnp.int32)
    for there in (beyond_y, *beside_x):
        greet({"win": there})
    greet({"chan": mate})
    for fetch in fetches[2:]:
        fetch.start()

    fetches[0].wait()
    fetches[1].wait()
    x = x_ref[0].astype(jnp.float32)
    pieces = jnp.concatenate([x[:, N2 * n1 : N2 * (n1 + 1)] for n1 in range(N1)], axis=0)
    s = jnp.dot(first_ref[...], pieces.astype(jnp.bfloat16), preferred_element_type=jnp.float32)
    s_re, s_im = s[: K1 * C], s[K1 * C :]
    fetches[2].wait()
    fetches[3].wait()
    t_re, t_im = twiddle_ref[0], twiddle_ref[1]
    y_re = (s_re * t_re - s_im * t_im).astype(jnp.bfloat16)
    y_im = (s_re * t_im + s_im * t_re).astype(jnp.bfloat16)
    spec = jnp.dot(
        jnp.concatenate([y_re, y_im], axis=1),
        jnp.concatenate([second_ref[0], second_ref[1]], axis=1),
        preferred_element_type=jnp.float32,
    )
    energy = spec[:, :K2] * spec[:, :K2] + spec[:, K2:] * spec[:, K2:]
    energy = jnp.sum(energy.reshape(K1, C, K2), axis=0)
    energy = energy + pltpu.roll(energy, 64, 1)
    energy = energy + pltpu.roll(energy, 32, 1)
    row = lax.broadcasted_iota(jnp.int32, (C, K2), 0)
    live = jnp.zeros((C, K2), jnp.float32)
    fetches[4].wait()
    for c in range(C):
        live = jnp.where(row == c, live_ref[c].astype(jnp.float32), live)
    factor = (1.0 / jnp.sqrt(energy * (1.0 / WB) + 1e-6)) * live
    factor = jnp.broadcast_to(factor[None], (K1, C, K2)).reshape(K1 * C, K2)
    white_re = (spec[:, :K2] * factor).astype(jnp.bfloat16)
    white_im = (spec[:, K2:] * factor).astype(jnp.bfloat16)
    halo[own, 0] = white_re
    halo[own, 1] = white_im

    pl.semaphore_wait(barrier, greeted)

    far_plane = 2 + 2 * towards
    slot_of = {
        place: PLANE * place[0] + (r if place[1] == SAME else beside + core) for place in PLACES[:-1]
    }
    slot_of[FAR] = PLANE * far_plane + beside + core
    to_mate = mate - j
    arrives = {place: has[place[0]] for place in PLACES[:-1]}
    arrives[FAR] = (has[0] & (y == 0)) | (has[4] & (y == 1))
    passed_on, from_mate = dict(arrives), dict(arrives)
    passed_on[0, SAME] = has[0] & (core == 1)
    from_mate[0, SAME] = has[0] & (core == 0)
    passed_on[4, SAME] = has[4] & (core == 0)
    from_mate[4, SAME] = has[4] & (core == 1)
    pair_of = {place: slot_of[place] + to_mate for place in PLACES}
    pair_of[0, SAME] = slot_of[0, SAME] + jnp.where(core == 0, to_mate, 0)
    pair_of[4, SAME] = slot_of[4, SAME] + jnp.where(core == 1, to_mate, 0)

    def out_copy(place):
        up, there, _ = targets[place]
        return pltpu.make_async_remote_copy(
            src_ref=halo.at[own],
            dst_ref=halo.at[own - PLANE * up],
            send_sem=halo_send.at[ISSUE.index(place)],
            recv_sem=halo_recv.at[own - PLANE * up],
            device_id={"chan": there + PLANE * up},
            device_id_type=MESH,
        )

    inside = has[1] & has[3]
    relays = {
        (1, SAME): (1, inside),
        (3, SAME): (-1, inside),
        (1, ACROSS): (1, inside & (y == 0)),
        (3, ACROSS): (-1, inside & (y == 1)),
        (2, ACROSS): (towards, has_t1),
    }

    def relay_copy(slot, up):
        return pltpu.make_async_remote_copy(
            src_ref=halo.at[slot],
            dst_ref=halo.at[slot - PLANE * up],
            send_sem=relay_send.at[slot],
            recv_sem=halo_recv.at[slot - PLANE * up],
            device_id={"chan": j + PLANE * up},
            device_id_type=MESH,
        )

    def mate_copy(slot):
        return pltpu.make_async_remote_copy(
            src_ref=halo.at[slot],
            dst_ref=halo.at[slot],
            send_sem=mate_send.at[slot],
            recv_sem=halo_recv.at[slot],
            device_id={"chan": mate},
            device_id_type=MESH,
        )

    for place in ISSUE:
        pl.when(targets[place][2])(lambda: out_copy(place).start())
    mate_copy(own).start()

    def tell(semaphore, there):
        pl.semaphore_signal(semaphore, inc=1, device_id={"win": there}, device_id_type=MESH)

    for there in beside_x:
        tell(row_in, there)

    for plane in (0, 1, 3, 4):

        @pl.when(jnp.logical_not(exists(plane)))
        def _():
            def clear(rank, _):
                halo[PLANE * plane + rank] = jnp.zeros((2, K1 * C, K2), jnp.bfloat16)
                return 0

            lax.fori_loop(0, PLANE, clear, 0)

    ownb[0] = jnp.broadcast_to(white_re.astype(jnp.float32)[:, None, :], (K1 * C, 8, K2))
    ownb[1] = jnp.broadcast_to(white_im.astype(jnp.float32)[:, None, :], (K1 * C, 8, K2))
    fetches[5].wait()

    def cross_terms(slots):
        total = jnp.zeros((64 * len(slots), LAGS), jnp.float32)
        for pair in range(K1 // 2):
            rows = slice(16 * pair, 16 * pair + 16)
            blocks = [
                (
                    halo[slot, 0, rows].astype(jnp.float32),
                    halo[slot, 1, rows].astype(jnp.float32),
                )
                for slot in slots
            ]
            for half in (0, 1):
                k1 = 2 * pair + half
                own_re, own_im = ownb[0, C * k1 : C * k1 + C], ownb[1, C * k1 : C * k1 + C]
                parts = []
                for block_re, block_im in blocks:
                    p_re = block_re[8 * half : 8 * half + 8][None]
                    p_im = block_im[8 * half : 8 * half + 8][None]
                    re = own_re * p_re + own_im * p_im
                    im = own_im * p_re - own_re * p_im
                    parts.append(
                        jnp.concatenate([re.reshape(64, K2), im.reshape(64, K2)], axis=1)
                    )
                cross = jnp.concatenate(parts, axis=0).astype(jnp.bfloat16)
                total += jnp.dot(cross, lag_ref[k1], preferred_element_type=jnp.float32)
        for index, slot in enumerate(slots):
            for c in range(C):
                value = total[64 * index + 8 * c : 64 * index + 8 * c + 8]
                acc[pl.ds(8 * (slot - r) + 7 - c, 8), c, :] = value

    def group_start(g):
        return group * g + 7 + (g >= wins // 2).astype(jnp.int32)

    def sums_copy(g):
        return pltpu.make_async_remote_copy(
            src_ref=sums_out.at[g],
            dst_ref=sums_in.at[w],
            send_sem=sums_send.at[g],
            recv_sem=sums_recv.at[w],
            device_id={"win": g},
            device_id_type=MESH,
        )

    def send_sums(first_group, count, turned=True):
        def one(index, _):
            g = first_group + (lax.rem(w + index, count) if turned else index)

            @pl.when(g != w)
            def _():
                value = acc[pl.ds(group_start(g), group)]
                sums_out[g] = value.reshape(group * C, LAGS).astype(jnp.bfloat16)
                sums_copy(g).start()

            return 0

        lax.fori_loop(0, count, one, 0)

    def from_chip(place):
        pl.when(arrives[place])(lambda: mate_copy(slot_of[place]).wait_recv())
        if place in relays:
            pl.when(relays[place][1])(lambda: relay_copy(slot_of[place], relays[place][0]).start())
        pl.when(passed_on[place])(lambda: mate_copy(slot_of[place]).start())

    def from_core(place):
        pl.when(from_mate[place])(lambda: mate_copy(slot_of[place] + to_mate).wait_recv())

    def rest_is_in():
        pl.semaphore_wait(rest_in, 1)

    def row_is_in():
        pl.semaphore_wait(row_in, 2)
        tell(rest_in, beyond_y)

    chip, core_of, sums = (
        lambda *places: [functools.partial(from_chip, place) for place in places],
        lambda place: [functools.partial(from_core, place)],
        lambda first, count: [functools.partial(send_sums, first, count)],
    )
    steps = (
        [(2, ACROSS), (1, SAME), (1, ACROSS), (3, SAME), (0, SAME), FAR, (3, ACROSS), (4, SAME)],
        [(2, ACROSS), (3, SAME), (3, ACROSS), (1, SAME), (1, ACROSS), (0, SAME), (4, SAME), FAR],
    )
    before = (
        {
            1: [row_is_in, *chip((1, SAME), (1, ACROSS), (2, ACROSS), (3, SAME))],
            4: [rest_is_in, *sums(2, 3)],
            5: [*chip((0, SAME)), *sums(5, 1)],
            6: chip(FAR, (3, ACROSS)),
            7: [functools.partial(send_sums, 0, 2, turned=False), *chip((4, SAME))],
            8: sums(6, 1),
        },
        {
            1: [row_is_in, *chip((3, SAME), (3, ACROSS), (2, ACROSS), (1, SAME))],
            4: [*chip((1, ACROSS)), rest_is_in, *sums(3, 3)],
            6: [*chip((0, SAME)), *sums(1, 2), *chip((4, SAME))],
            7: [*sums(0, 1), *chip(FAR)],
        },
    )

    def event(u, column):
        if u == 0:
            mate_copy(own + to_mate).wait_recv()
        else:
            for act in [*before[column].get(u, []), *core_of(steps[column][u - 1])]:
                act()

    def before_step(u):
        for column in (0, 1):
            pl.when(y == column)(functools.partial(event, u, column))

    units = [(own, own + to_mate)]
    units += [
        tuple(jnp.where(y == 0, table[a], table[b]) for table in (slot_of, pair_of))
        for a, b in zip(*steps, strict=True)
    ]
    events = {u: functools.partial(before_step, u) for u in range(len(units))}

    def pick(u, values):
        chosen = values[0]
        for index in range(1, len(values)):
            chosen = jnp.where(u == index, values[index], chosen)
        return chosen

    def unit(u, _):
        for at, event in events.items():
            pl.when(u == at)(event)
        cross_terms([pick(u, [a for a, _ in units]), pick(u, [b for _, b in units])])
        return 0

    lax.fori_loop(0, len(units), unit, 0)

    send_sums(7, 1)
    send_sums(6, y)

    out_ref[...] = acc[pl.ds(group_start(w), group)]
    for place in relays:
        pl.when(relays[place][1])(lambda: relay_copy(slot_of[place], relays[place][0]).wait_send())
    for place in targets:
        pl.when(targets[place][2])(lambda: out_copy(place).wait_send())
    for place in PLACES:
        pl.when(passed_on[place])(lambda: mate_copy(slot_of[place]).wait_send())
    mate_copy(own).wait_send()

    def sent_sums(step, _):
        sums_copy(lax.rem(w + step, wins)).wait_send()
        return 0

    lax.fori_loop(1, wins, sent_sums, 0)

    def gather(step, _):
        source = lax.rem(w + step, wins)
        pltpu.make_async_remote_copy(
            src_ref=sums_out.at[source],
            dst_ref=sums_in.at[source],
            send_sem=sums_send.at[source],
            recv_sem=sums_recv.at[source],
            device_id={"win": source},
            device_id_type=MESH,
        ).wait_recv()
        out_ref[...] += sums_in[source].astype(jnp.float32).reshape(group, C, LAGS)
        return 0

    lax.fori_loop(1, wins, gather, 0)


def solution(mesh):
    chans, wins = mesh.shape["chan"], mesh.shape["win"]
    group = BAND // wins

    def local(recordings, channel_live):
        constants = tables(wins * recordings.shape[0])
        operands = (channel_live, recordings, *constants)
        operands = [pltpu.with_memory_space_constraint(array, pltpu.HBM) for array in operands]

        def body(*refs):
            kernel(chans, wins, *refs)

        copies = [pltpu.SMEM(channel_live.shape, channel_live.dtype)]
        copies += [pltpu.VMEM(array.shape, array.dtype) for array in operands[1:]]
        return pl.pallas_call(
            body,
            out_shape=pltpu.VMEM((group, C, LAGS), jnp.float32),
            in_specs=[pl.BlockSpec(memory_space=pltpu.HBM)] * len(operands),
            out_specs=pl.BlockSpec(memory_space=pltpu.VMEM),
            scratch_shapes=[
                *copies,
                pltpu.VMEM((SLOTS, 2, K1 * C, K2), jnp.bfloat16),
                pltpu.VMEM((2, K1 * C, 8, K2), jnp.float32),
                pltpu.VMEM((BAND + 16, C, LAGS), jnp.float32),
                pltpu.VMEM((wins, group * C, LAGS), jnp.bfloat16),
                pltpu.VMEM((wins, group * C, LAGS), jnp.bfloat16),
                pltpu.SemaphoreType.DMA((len(operands),)),
                pltpu.SemaphoreType.DMA((8,)),
                pltpu.SemaphoreType.DMA((SLOTS,)),
                pltpu.SemaphoreType.DMA((SLOTS,)),
                pltpu.SemaphoreType.DMA((SLOTS,)),
                pltpu.SemaphoreType.DMA((wins,)),
                pltpu.SemaphoreType.DMA((wins,)),
                pltpu.SemaphoreType.REGULAR,
                pltpu.SemaphoreType.REGULAR,
            ],
            compiler_params=pltpu.CompilerParams(
                collective_id=0, has_side_effects=True, vmem_limit_bytes=24 * 1024 * 1024
            ),
            name="correlate",
        )(*operands)

    return jax.shard_map(
        local,
        mesh=mesh,
        in_specs=(P("win", "chan", None), P("chan")),
        out_specs=P("win", "chan", None),
        check_vma=False,
    )
```

```python
import functools
import math

import jax
import jax.numpy as jnp
import numpy as np
from jax import lax
from jax.experimental import pallas as pl
from jax.experimental.pallas import tpu as pltpu
from jax.sharding import PartitionSpec as P

NT = 4096
NF = 2048
WB = 64
BAND = 128
LAGS = 128
C = 8
N1 = 16
N2 = 256
K1 = 16
K2 = 128
PLANE = 4
WIN_X = 4
PLANES = 5
SLOTS = PLANE * PLANES
MESH = pl.DeviceIdType.MESH
SAME, ACROSS = "same", "across"
T1, A1, HERE = "t1", "a1", "here"
ISSUE = [(T1, ACROSS), (HERE, ACROSS), (T1, SAME), (A1, SAME)]
FAR = "far"
PLACES = [(2, ACROSS), (1, SAME), (1, ACROSS), (3, SAME), (3, ACROSS), (0, SAME), (4, SAME), FAR]

def bin_order():
    lane = np.arange(K2)
    return 4 * (lane % 32) + lane // 32


def tables(window_count):
    tau = 2.0 * math.pi
    k1, n1, n2 = np.arange(K1), np.arange(N1), np.arange(N2)
    k2 = bin_order()
    first = tau * (np.outer(k1, n1) % 16) / 16.0
    first = np.concatenate([np.cos(first), -np.sin(first)], axis=0)
    first = np.kron(first, np.eye(C))
    twiddle = tau * (np.outer(k1, n2) % NT) / NT
    twiddle = np.stack([np.cos(twiddle), -np.sin(twiddle)])
    twiddle = np.repeat(twiddle, C, axis=1)
    second = tau * (np.outer(n2, k2) % N2) / N2
    cos, sin = np.cos(second), np.sin(second)
    second = np.stack([np.concatenate([cos, sin]), np.concatenate([-sin, cos])])
    bins = k1[:, None] + K1 * k2[None, :]
    lag = tau * ((bins[:, :, None] * (np.arange(LAGS) - LAGS // 2)) % NT) / NT
    factor = 1.0 / math.sqrt(window_count * NF)
    lag = np.concatenate([np.cos(lag) * factor, -np.sin(lag) * factor], axis=1)
    return (
        jnp.asarray(first, jnp.bfloat16),
        jnp.asarray(twiddle, jnp.float32),
        jnp.asarray(second, jnp.bfloat16),
        jnp.asarray(lag, jnp.bfloat16),
    )


def kernel(
    chans,
    wins,
    live_hbm,
    x_hbm,
    first_hbm,
    twiddle_hbm,
    second_hbm,
    lag_hbm,
    out_ref,
    live_ref,
    x_ref,
    first_ref,
    twiddle_ref,
    second_ref,
    lag_ref,
    halo,
    ownb,
    acc,
    sums_out,
    sums_in,
    fetch_sem,
    halo_send,
    mate_send,
    relay_send,
    halo_recv,
    sums_send,
    sums_recv,
    row_in,
    rest_in,
):
    j = lax.axis_index("chan")
    w = lax.axis_index("win")
    group = BAND // wins
    planes = chans // PLANE
    z, r = j // PLANE, j % PLANE
    y, core = r // 2, r % 2
    beside = 2 - 2 * y
    own = 2 * PLANE + r

    fetches = [
        pltpu.make_async_copy(source, target, fetch_sem.at[index])
        for index, (source, target) in enumerate(
            (
                (x_hbm, x_ref),
                (first_hbm, first_ref),
                (twiddle_hbm, twiddle_ref),
                (second_hbm, second_ref),
                (live_hbm, live_ref),
                (lag_hbm, lag_ref),
            )
        )
    ]

    def exists(plane):
        there = z + plane - 2
        return (there >= 0) & (there < planes)

    side, mate = j + 2 - 4 * y, j + 1 - 2 * core
    towards = 2 * y - 1
    always = j >= 0
    has = [exists(plane) for plane in range(PLANES)]
    has_t1, has_a1 = (has[1] & (y == 0)) | (has[3] & (y == 1)), (has[3] & (y == 0)) | (has[1] & (y == 1))
    targets = {
        (T1, ACROSS): (towards, side, has_t1),
        (T1, SAME): (-towards, j, has_a1),
        (A1, SAME): (towards, j, has_t1),
        (HERE, ACROSS): (0, side, always),
    }

    fetches[0].start()
    fetches[1].start()
    barrier = pltpu.get_barrier_semaphore()

    def greet(there):
        pl.semaphore_signal(barrier, inc=1, device_id=there, device_id_type=MESH)

    row, row_width = w // WIN_X * WIN_X, WIN_X
    beside_x = [row + lax.rem(w + step, row_width) for step in (1, row_width - 1)]
    beyond_y = lax.rem(w + WIN_X, wins)
    greeted = 1 + 3
    for up, there, present in targets.values():
        pl.when(present)(lambda: greet({"chan": there + PLANE * up}))
        greeted += present.astype(jnp.int32)
    for there in (beyond_y, *beside_x):
        greet({"win": there})
    greet({"chan": mate})
    for fetch in fetches[2:]:
        fetch.start()

    fetches[0].wait()
    fetches[1].wait()
    x = x_ref[0].astype(jnp.float32)
    pieces = jnp.concatenate([x[:, N2 * n1 : N2 * (n1 + 1)] for n1 in range(N1)], axis=0)
    s = jnp.dot(first_ref[...], pieces.astype(jnp.bfloat16), preferred_element_type=jnp.float32)
    s_re, s_im = s[: K1 * C], s[K1 * C :]
    fetches[2].wait()
    fetches[3].wait()
    t_re, t_im = twiddle_ref[0], twiddle_ref[1]
    y_re = (s_re * t_re - s_im * t_im).astype(jnp.bfloat16)
    y_im = (s_re * t_im + s_im * t_re).astype(jnp.bfloat16)
    spec = jnp.dot(
        jnp.concatenate([y_re, y_im], axis=1),
        jnp.concatenate([second_ref[0], second_ref[1]], axis=1),
        preferred_element_type=jnp.float32,
    )
    energy = spec[:, :K2] * spec[:, :K2] + spec[:, K2:] * spec[:, K2:]
    energy = jnp.sum(energy.reshape(K1, C, K2), axis=0)
    energy = energy + pltpu.roll(energy, 64, 1)
    energy = energy + pltpu.roll(energy, 32, 1)
    row = lax.broadcasted_iota(jnp.int32, (C, K2), 0)
    live = jnp.zeros((C, K2), jnp.float32)
    fetches[4].wait()
    for c in range(C):
        live = jnp.where(row == c, live_ref[c].astype(jnp.float32), live)
    factor = (1.0 / jnp.sqrt(energy * (1.0 / WB) + 1e-6)) * live
    factor = jnp.broadcast_to(factor[None], (K1, C, K2)).reshape(K1 * C, K2)
    white_re = (spec[:, :K2] * factor).astype(jnp.bfloat16)
    white_im = (spec[:, K2:] * factor).astype(jnp.bfloat16)
    halo[own, 0] = white_re
    halo[own, 1] = white_im

    pl.semaphore_wait(barrier, greeted)

    far_plane = 2 + 2 * towards
    slot_of = {
        place: PLANE * place[0] + (r if place[1] == SAME else beside + core) for place in PLACES[:-1]
    }
    slot_of[FAR] = PLANE * far_plane + beside + core
    to_mate = mate - j
    arrives = {place: has[place[0]] for place in PLACES[:-1]}
    arrives[FAR] = (has[0] & (y == 0)) | (has[4] & (y == 1))
    passed_on, from_mate = dict(arrives), dict(arrives)
    passed_on[0, SAME] = has[0] & (core == 1)
    from_mate[0, SAME] = has[0] & (core == 0)
    passed_on[4, SAME] = has[4] & (core == 0)
    from_mate[4, SAME] = has[4] & (core == 1)
    pair_of = {place: slot_of[place] + to_mate for place in PLACES}
    pair_of[0, SAME] = slot_of[0, SAME] + jnp.where(core == 0, to_mate, 0)
    pair_of[4, SAME] = slot_of[4, SAME] + jnp.where(core == 1, to_mate, 0)

    def out_copy(place):
        up, there, _ = targets[place]
        return pltpu.make_async_remote_copy(
            src_ref=halo.at[own],
            dst_ref=halo.at[own - PLANE * up],
            send_sem=halo_send.at[ISSUE.index(place)],
            recv_sem=halo_recv.at[own - PLANE * up],
            device_id={"chan": there + PLANE * up},
            device_id_type=MESH,
        )

    inside = has[1] & has[3]
    relays = {
        (1, SAME): (1, inside),
        (3, SAME): (-1, inside),
        (1, ACROSS): (1, inside & (y == 0)),
        (3, ACROSS): (-1, inside & (y == 1)),
        (2, ACROSS): (towards, has_t1),
    }

    def relay_copy(slot, up):
        return pltpu.make_async_remote_copy(
            src_ref=halo.at[slot],
            dst_ref=halo.at[slot - PLANE * up],
            send_sem=relay_send.at[slot],
            recv_sem=halo_recv.at[slot - PLANE * up],
            device_id={"chan": j + PLANE * up},
            device_id_type=MESH,
        )

    def mate_copy(slot):
        return pltpu.make_async_remote_copy(
            src_ref=halo.at[slot],
            dst_ref=halo.at[slot],
            send_sem=mate_send.at[slot],
            recv_sem=halo_recv.at[slot],
            device_id={"chan": mate},
            device_id_type=MESH,
        )

    for place in ISSUE:
        pl.when(targets[place][2])(lambda: out_copy(place).start())
    mate_copy(own).start()

    def tell(semaphore, there):
        pl.semaphore_signal(semaphore, inc=1, device_id={"win": there}, device_id_type=MESH)

    for there in beside_x:
        tell(row_in, there)

    for plane in (0, 1, 3, 4):

        @pl.when(jnp.logical_not(exists(plane)))
        def _():
            def clear(rank, _):
                halo[PLANE * plane + rank] = jnp.zeros((2, K1 * C, K2), jnp.bfloat16)
                return 0

            lax.fori_loop(0, PLANE, clear, 0)

    ownb[0] = jnp.broadcast_to(white_re.astype(jnp.float32)[:, None, :], (K1 * C, 8, K2))
    ownb[1] = jnp.broadcast_to(white_im.astype(jnp.float32)[:, None, :], (K1 * C, 8, K2))
    fetches[5].wait()

    def cross_terms(slots):
        total = jnp.zeros((64 * len(slots), LAGS), jnp.float32)
        for pair in range(K1 // 2):
            rows = slice(16 * pair, 16 * pair + 16)
            blocks = [
                (
                    halo[slot, 0, rows].astype(jnp.float32),
                    halo[slot, 1, rows].astype(jnp.float32),
                )
                for slot in slots
            ]
            for half in (0, 1):
                k1 = 2 * pair + half
                own_re, own_im = ownb[0, C * k1 : C * k1 + C], ownb[1, C * k1 : C * k1 + C]
                parts = []
                for block_re, block_im in blocks:
                    p_re = block_re[8 * half : 8 * half + 8][None]
                    p_im = block_im[8 * half : 8 * half + 8][None]
                    re = own_re * p_re + own_im * p_im
                    im = own_im * p_re - own_re * p_im
                    parts.append(
                        jnp.concatenate([re.reshape(64, K2), im.reshape(64, K2)], axis=1)
                    )
                cross = jnp.concatenate(parts, axis=0).astype(jnp.bfloat16)
                total += jnp.dot(cross, lag_ref[k1], preferred_element_type=jnp.float32)
        for index, slot in enumerate(slots):
            for c in range(C):
                value = total[64 * index + 8 * c : 64 * index + 8 * c + 8]
                acc[pl.ds(8 * (slot - r) + 7 - c, 8), c, :] = value

    def group_start(g):
        return group * g + 7 + (g >= wins // 2).astype(jnp.int32)

    def sums_copy(g):
        return pltpu.make_async_remote_copy(
            src_ref=sums_out.at[g],
            dst_ref=sums_in.at[w],
            send_sem=sums_send.at[g],
            recv_sem=sums_recv.at[w],
            device_id={"win": g},
            device_id_type=MESH,
        )

    def send_sums(first_group, count, turned=True):
        def one(index, _):
            g = first_group + (lax.rem(w + index, count) if turned else index)

            @pl.when(g != w)
            def _():
                value = acc[pl.ds(group_start(g), group)]
                sums_out[g] = value.reshape(group * C, LAGS).astype(jnp.bfloat16)
                sums_copy(g).start()

            return 0

        lax.fori_loop(0, count, one, 0)

    def from_chip(place):
        pl.when(arrives[place])(lambda: mate_copy(slot_of[place]).wait_recv())
        if place in relays:
            pl.when(relays[place][1])(lambda: relay_copy(slot_of[place], relays[place][0]).start())
        pl.when(passed_on[place])(lambda: mate_copy(slot_of[place]).start())

    def from_core(place):
        pl.when(from_mate[place])(lambda: mate_copy(slot_of[place] + to_mate).wait_recv())

    def rest_is_in():
        pl.semaphore_wait(rest_in, 1)

    def row_is_in():
        pl.semaphore_wait(row_in, 2)
        tell(rest_in, beyond_y)

    chip, core_of, sums = (
        lambda *places: [functools.partial(from_chip, place) for place in places],
        lambda place: [functools.partial(from_core, place)],
        lambda first, count: [functools.partial(send_sums, first, count)],
    )
    steps = (
        [(2, ACROSS), (1, SAME), (1, ACROSS), (3, SAME), (0, SAME), FAR, (3, ACROSS), (4, SAME)],
        [(2, ACROSS), (3, SAME), (3, ACROSS), (1, SAME), (1, ACROSS), (0, SAME), (4, SAME), FAR],
    )
    before = (
        {
            1: [row_is_in, *chip((1, SAME), (2, ACROSS), (1, ACROSS), (3, SAME))],
            4: [rest_is_in, *sums(2, 3)],
            5: [*chip((0, SAME)), *sums(5, 1)],
            6: chip(FAR, (3, ACROSS)),
            7: [functools.partial(send_sums, 0, 2, turned=False), *chip((4, SAME))],
            8: sums(6, 1),
        },
        {
            1: [row_is_in, *chip((3, SAME), (2, ACROSS), (3, ACROSS), (1, SAME))],
            4: [*chip((1, ACROSS)), rest_is_in, *sums(3, 3)],
            6: [*chip((0, SAME)), *sums(1, 2), *chip((4, SAME))],
            7: [*sums(0, 1), *chip(FAR)],
        },
    )

    def event(u, column):
        if u == 0:
            mate_copy(own + to_mate).wait_recv()
        else:
            for act in [*before[column].get(u, []), *core_of(steps[column][u - 1])]:
                act()

    def before_step(u):
        for column in (0, 1):
            pl.when(y == column)(functools.partial(event, u, column))

    units = [(own, own + to_mate)]
    units += [
        tuple(jnp.where(y == 0, table[a], table[b]) for table in (slot_of, pair_of))
        for a, b in zip(*steps, strict=True)
    ]
    events = {u: functools.partial(before_step, u) for u in range(len(units))}

    def pick(u, values):
        chosen = values[0]
        for index in range(1, len(values)):
            chosen = jnp.where(u == index, values[index], chosen)
        return chosen

    def unit(u, _):
        for at, event in events.items():
            pl.when(u == at)(event)
        cross_terms([pick(u, [a for a, _ in units]), pick(u, [b for _, b in units])])
        return 0

    lax.fori_loop(0, len(units), unit, 0)

    send_sums(7, 1)
    send_sums(6, y)

    out_ref[...] = acc[pl.ds(group_start(w), group)]
    for place in relays:
        pl.when(relays[place][1])(lambda: relay_copy(slot_of[place], relays[place][0]).wait_send())
    for place in targets:
        pl.when(targets[place][2])(lambda: out_copy(place).wait_send())
    for place in PLACES:
        pl.when(passed_on[place])(lambda: mate_copy(slot_of[place]).wait_send())
    mate_copy(own).wait_send()

    def sent_sums(step, _):
        sums_copy(lax.rem(w + step, wins)).wait_send()
        return 0

    lax.fori_loop(1, wins, sent_sums, 0)

    def gather(step, _):
        source = lax.rem(w + step, wins)
        pltpu.make_async_remote_copy(
            src_ref=sums_out.at[source],
            dst_ref=sums_in.at[source],
            send_sem=sums_send.at[source],
            recv_sem=sums_recv.at[source],
            device_id={"win": source},
            device_id_type=MESH,
        ).wait_recv()
        out_ref[...] += sums_in[source].astype(jnp.float32).reshape(group, C, LAGS)
        return 0

    lax.fori_loop(1, wins, gather, 0)


def solution(mesh):
    chans, wins = mesh.shape["chan"], mesh.shape["win"]
    group = BAND // wins

    def local(recordings, channel_live):
        constants = tables(wins * recordings.shape[0])
        operands = (channel_live, recordings, *constants)
        operands = [pltpu.with_memory_space_constraint(array, pltpu.HBM) for array in operands]

        def body(*refs):
            kernel(chans, wins, *refs)

        copies = [pltpu.SMEM(channel_live.shape, channel_live.dtype)]
        copies += [pltpu.VMEM(array.shape, array.dtype) for array in operands[1:]]
        return pl.pallas_call(
            body,
            out_shape=pltpu.VMEM((group, C, LAGS), jnp.float32),
            in_specs=[pl.BlockSpec(memory_space=pltpu.HBM)] * len(operands),
            out_specs=pl.BlockSpec(memory_space=pltpu.VMEM),
            scratch_shapes=[
                *copies,
                pltpu.VMEM((SLOTS, 2, K1 * C, K2), jnp.bfloat16),
                pltpu.VMEM((2, K1 * C, 8, K2), jnp.float32),
                pltpu.VMEM((BAND + 16, C, LAGS), jnp.float32),
                pltpu.VMEM((wins, group * C, LAGS), jnp.bfloat16),
                pltpu.VMEM((wins, group * C, LAGS), jnp.bfloat16),
                pltpu.SemaphoreType.DMA((len(operands),)),
                pltpu.SemaphoreType.DMA((8,)),
                pltpu.SemaphoreType.DMA((SLOTS,)),
                pltpu.SemaphoreType.DMA((SLOTS,)),
                pltpu.SemaphoreType.DMA((SLOTS,)),
                pltpu.SemaphoreType.DMA((wins,)),
                pltpu.SemaphoreType.DMA((wins,)),
                pltpu.SemaphoreType.REGULAR,
                pltpu.SemaphoreType.REGULAR,
            ],
            compiler_params=pltpu.CompilerParams(
                collective_id=0, has_side_effects=True, vmem_limit_bytes=24 * 1024 * 1024
            ),
            name="correlate",
        )(*operands)

    return jax.shard_map(
        local,
        mesh=mesh,
        in_specs=(P("win", "chan", None), P("chan")),
        out_specs=P("win", "chan", None),
        check_vma=False,
    )
```
